32 devices in a mesh: dp: 2 (over x), expert: 16 (over z, y, core).
Axes of the slice: x: 2, y: 2, z: 4, core: 2. Of those that a mesh axis runs over, the one named last changes fastest.
Arguments:
- tokens: bfloat16 [2048, 3584], P('expert'), may hold values from -6 to 6
- expert_ids: int32 [2048, 8], P('expert'), may hold values from 0 to 15, all different within a row; in each aligned block of 128 rows (0 to 127, 128 to 255, ...) at most 96 rows name the same one
- route_weight: float32 [2048, 8], P('expert'), may hold values from 0.1 to 1
- pair_swap: int32 [8], replicated, may hold values from 0 to 1, as said below
- expert_gate: bfloat16 [16, 3584, 2048], P('expert', None, 'dp'), may hold values from -0.09375 to 0.09375
- expert_up: bfloat16 [16, 3584, 2048], P('expert', None, 'dp'), may hold values from -0.09375 to 0.09375
- expert_down: bfloat16 [16, 2048, 3584], P('expert', 'dp'), may hold values from -0.1875 to 0.1875
- shared_gate: bfloat16 [3584, 2048], P(None, 'dp'), may hold values from -0.09375 to 0.09375
- shared_up: bfloat16 [3584, 2048], P(None, 'dp'), may hold values from -0.09375 to 0.09375
- shared_down: bfloat16 [2048, 3584], P('dp'), may hold values from -0.1875 to 0.1875
Outputs:
- layer_out: bfloat16 [2048, 3584], P('expert', 'dp')
The draws below stay inside these ranges and needn't reach their ends.
Inputs may be any that keep to these rules, and one draw needn't show every extreme that they name: `expert_ids`: each row names 8 different experts; within the rows of one device (aligned blocks of 128 rows) no expert is named more than 96 times, a bound that some block reaches. `pair_swap`: entry 0 is always 1; the other entries are 0 or 1.
All inputs are finite; a program needn't handle non-finite values.
Results may differ from the reference program's by a relative error of at most 0.012.
Values may be sent and summed in bfloat16 or wider, within the bound.
No kernel may reach another device: no remote copies, remote signals or barrier semaphores. Data moves between devices by JAX's collectives and lax.ppermute only.
A program may use at most 192 MiB of HBM per device.

```python
import math
import jax
import jax.numpy as jnp
import numpy as np
from jax import lax

D = 3584
HIDDEN_SIZE = 2048
TOPK = 8
TOK_DEV = 128
EXPERTS = 16
HID_DEV = 1024
MOST = 96
TOKENS = 2048
N_DP = 2
N_EXPERT = 16


def draw_pair_swap(key, part):
    flags = jax.random.randint(key, (EXPERTS // 2,), 0, 2).astype(jnp.int32)
    return flags.at[0].set(1)


def spiked(result, own_key, source, target, shards_of, factor):
    def block_of(dim):
        return (jnp.arange(result.shape[dim]) // (result.shape[dim] // shards_of)).reshape((-1,) + (1,) * (result.ndim - 1 - dim))

    first = jax.random.permutation(own_key, shards_of)[block_of(target)]
    second = (block_of(target) + shards_of // 2) % shards_of
    return jnp.where((block_of(source) == first) | (block_of(source) == second), factor * result, result)


def block_levels(rng, shape, cuts, smallest, high):
    def one(axis_at, blocks):
        steps = jax.random.uniform(jax.random.fold_in(jax.random.fold_in(rng, 6), axis_at), (blocks,), jnp.float32, smallest / len(cuts), high / len(cuts))
        return jnp.repeat(jnp.exp(steps), shape[axis_at] // blocks).reshape((-1,) + (1,) * (len(shape) - axis_at - 1))

    factor_of = one(*cuts[0])
    for cut in cuts[1:]:
        factor_of = factor_of * one(*cut)
    return factor_of


def assign_block(own_key, own, number, rows, number_of, top, reach, slope):
    order = jax.random.permutation(own_key, number_of)
    crowded, ordinary = load_shares(number_of, rows * top, reach, slope, True), load_shares(number_of, rows * top, reach, slope, False)
    places = jnp.arange(number_of)

    def named(lengths, rotation):
        used = int((lengths > 0).sum())
        fixed = max(1, used // 4)
        passed = fixed + (places - fixed + rotation * (used - fixed)) % max(1, number_of - fixed)
        return jnp.zeros((number_of,), jnp.int32).at[order[jnp.where(places < fixed, places, passed)]].set(jnp.asarray(lengths, jnp.int32))

    lengths = jnp.where(number % 4 == 0, named(crowded, number // 4), named(ordinary, number - number // 4 - 1))
    mixed = jax.random.permutation(jax.random.fold_in(own, 3), number_of)
    giver, receiver = mixed[0:number_of // 2 * 2:2], mixed[1:number_of // 2 * 2:2]
    slack = jnp.minimum(lengths[giver] - 1, reach - lengths[receiver]) // 2
    slack = jnp.where((giver == order[0]) | (receiver == order[0]) | (lengths[receiver] == 0), 0, jnp.maximum(slack, 0))
    passed = jax.random.randint(jax.random.fold_in(own, 4), (number_of // 2,), 0, 1 << 20) % (slack + 1)
    lengths = lengths.at[giver].add(-passed).at[receiver].add(passed)
    labels = jnp.searchsorted(jnp.cumsum(lengths), jnp.arange(rows * top), side="right").astype(jnp.int32)
    listing = labels.reshape(top, rows).T
    listing = listing[jax.random.permutation(jax.random.fold_in(own, 1), rows)]
    rotation = jax.random.randint(jax.random.fold_in(own, 2), (rows, 1), 0, top)
    return jnp.take_along_axis(listing, (jnp.arange(top)[None, :] + rotation) % top, axis=1)


def load_shares(count, total, most, slope, full):
    portions = [(1 << 20) // math.isqrt(rank ** slope) + 1 for rank in range(1, count + 1)]
    largest = most if full else min(most, max(-(-total // count), total * portions[0] // sum(portions)))
    least = 1 if total - largest >= count - 1 else 0
    counts, surplus = [largest] + [least] * (count - 1), total - largest - least * (count - 1)
    while surplus > 0:
        free = [i for i in range(1, count) if counts[i] < largest] or [i for i in range(1, count) if counts[i] < most]
        whole, remaining = sum([portions[i] for i in free]), surplus
        for i in free:
            extra = min(most - counts[i], max(1, remaining * portions[i] // whole), surplus)
            counts[i] = counts[i] + extra
            surplus = surplus - extra
    return np.array(counts)


def centred(key, shape, scale, limit, shards=(), held_as=jnp.bfloat16):
    result = scale * jax.random.normal(key, shape, jnp.float32)
    if shards:
        result = result * block_levels(key, shape, shards, -0.22, 0.18)
    return jnp.clip(result, -limit, limit).astype(held_as)


def gaussian_with(own_key, shape, width, limit, cuts, heavy, kind=jnp.bfloat16):
    result = width * jax.random.normal(own_key, shape, jnp.float32)
    if cuts:
        result = result * block_levels(own_key, shape, cuts, -0.22, 0.18)
    return jnp.clip(spiked(result, jax.random.fold_in(own_key, 3), *heavy), -limit, limit).astype(kind)


def setup_inputs(seed: int = 0) -> dict:
    arg_keys = jax.random.split(jax.random.key(seed), 11)
    tokens = centred(arg_keys[0], (TOKENS, D), 1.0, 6.0, ((0, 16),))
    expert_ids_keys = jax.random.split(jax.random.fold_in(arg_keys[1], 1), TOKENS // TOK_DEV)
    expert_ids_turns = jax.random.permutation(jax.random.fold_in(arg_keys[1], 3), TOKENS // TOK_DEV)
    expert_ids = jax.vmap(lambda own, number: assign_block(jax.random.fold_in(arg_keys[1], 2), own, number, TOK_DEV, EXPERTS, TOPK, MOST, 2))(expert_ids_keys, expert_ids_turns).reshape((TOKENS, TOPK))
    route_weight = jnp.clip(jnp.exp(math.log(1.0) - 2.3025851 * jax.random.uniform(arg_keys[2], (TOKENS, TOPK), jnp.float32) ** block_levels(arg_keys[2], (TOKENS, TOPK), ((0, 16),), -0.2, 0.2)), 0.1, 1.0)
    pair_swap = draw_pair_swap(jax.random.fold_in(arg_keys[10], 71), 0)
    expert_gate = centred(arg_keys[4], (EXPERTS, D, HIDDEN_SIZE), D ** -0.5, 0.09375, ((0, 16), (2, 2)))
    expert_up = centred(arg_keys[5], (EXPERTS, D, HIDDEN_SIZE), D ** -0.5, 0.09375, ((0, 16), (2, 2)))
    expert_down = gaussian_with(arg_keys[6], (EXPERTS, HIDDEN_SIZE, D), HIDDEN_SIZE ** -0.5, 0.1875, ((0, 16), (1, 2)), (1, 2, 2, 2.0))
    shared_gate = centred(arg_keys[7], (D, HIDDEN_SIZE), D ** -0.5, 0.09375, ((1, 2),))
    shared_up = centred(arg_keys[8], (D, HIDDEN_SIZE), D ** -0.5, 0.09375, ((1, 2),))
    shared_down = gaussian_with(arg_keys[9], (HIDDEN_SIZE, D), HIDDEN_SIZE ** -0.5, 0.1875, ((0, 2),), (0, 1, 2, 2.0))
    return {"tokens": tokens, "expert_ids": expert_ids, "route_weight": route_weight, "pair_swap": pair_swap, "expert_gate": expert_gate, "expert_up": expert_up, "expert_down": expert_down, "shared_gate": shared_gate, "shared_up": shared_up, "shared_down": shared_down}


def reference(tokens, expert_ids, route_weight, pair_swap, expert_gate, expert_up, expert_down, shared_gate, shared_up, shared_down):
    half_axis = EXPERTS // 2
    columns = jnp.arange(EXPERTS, dtype=jnp.int32)
    swap_flags = pair_swap[columns % half_axis]
    holder = jnp.where(swap_flags == 1, (columns + half_axis) % EXPERTS, columns).astype(jnp.int32)
    mix = route_weight / jnp.sum(route_weight, axis=1, keepdims=True)
    shared_gv = jnp.dot(tokens, shared_gate, preferred_element_type=jnp.float32)
    shared_uv = jnp.dot(tokens, shared_up, preferred_element_type=jnp.float32)
    shared_act = (jax.nn.silu(shared_gv) * shared_uv).astype(jnp.bfloat16)
    shared_out = jnp.dot(shared_act, shared_down, preferred_element_type=jnp.float32)
    flat_ids = expert_ids.reshape(-1)
    flat_mix = mix.reshape(-1)
    owner_row = (jnp.arange(TOKENS * TOPK, dtype=jnp.int32) // TOPK).astype(jnp.int32)
    capacity = N_EXPERT * MOST
    padded = jnp.concatenate([tokens, jnp.zeros((1, D), tokens.dtype)], axis=0)

    def accumulate(carry, expert):
        stored = holder[expert]
        chosen = (flat_ids == expert).astype(jnp.int32)
        before = jnp.cumsum(chosen) - chosen
        position = jnp.where(chosen == 1, before, capacity).astype(jnp.int32)
        rows_at = jnp.full((capacity + 1,), TOKENS, jnp.int32).at[position].set(owner_row)[:capacity]
        mix_at = jnp.zeros((capacity + 1,), jnp.float32).at[position].set(flat_mix)[:capacity]
        rows_in = padded[rows_at]
        gate_val = jnp.dot(rows_in, expert_gate[stored], preferred_element_type=jnp.float32)
        up_val = jnp.dot(rows_in, expert_up[stored], preferred_element_type=jnp.float32)
        act = (jax.nn.silu(gate_val) * up_val).astype(jnp.bfloat16)
        act_groups = act.reshape(capacity, N_DP, HID_DEV).astype(jnp.float32)
        down_groups = expert_down[stored].reshape(N_DP, HID_DEV, D).astype(jnp.float32)
        parts = jnp.einsum("cnh,nhd->ncd", act_groups, down_groups).astype(jnp.bfloat16)
        parts = lax.optimization_barrier(parts)
        summed = jnp.sum(parts.astype(jnp.float32), axis=0)
        carry = carry.at[rows_at].add(mix_at[:, None] * summed)
        return carry, None

    start = jnp.zeros((TOKENS + 1, D), jnp.float32)
    routed, _ = lax.scan(accumulate, start, jnp.arange(EXPERTS, dtype=jnp.int32))
    return (shared_out + 2.5 * routed[:TOKENS]).astype(jnp.bfloat16)
```

```python
import functools

import jax
import jax.numpy as jnp
from jax import lax
from jax.experimental import pallas as pl
from jax.experimental.pallas import tpu as pltpu
from jax.sharding import PartitionSpec as P

routed_scale = 2.5
LANES = 128
TILE = 256
VMEM = 52 * 1024 * 1024


def exchange(value, axis, mask):
    pairs = [(source, source ^ mask) for source in range(lax.axis_size(axis))]
    return lax.ppermute(value, axis, pairs)


def widen_body(experts, share, n_dp, info, tokens, ids, weight, rows, carried):
    count, width = tokens.shape
    rates = weight[...]
    rates = routed_scale * rates / jnp.sum(rates, axis=1, keepdims=True)
    lane = lax.broadcasted_iota(jnp.int32, (count, LANES), 1)
    total = jnp.zeros((count, LANES), jnp.float32)
    for choice in range(ids.shape[1]):
        total += jnp.where(ids[:, choice : choice + 1] == lane % experts, rates[:, choice : choice + 1], 0.0)
    high = total.astype(jnp.bfloat16).astype(jnp.float32)
    middle = (total - high).astype(jnp.bfloat16).astype(jnp.float32)
    low = total - high - middle
    term = lane // experts
    held = jnp.where(term == 0, high, jnp.where(term == 1, middle, jnp.where(term == 2, low, 0.0)))
    rows[:, :width] = tokens[...]
    rows[:, width:] = held.astype(jnp.bfloat16)
    if carried is not None:
        start = pl.multiple_of(info[0] * share, 16)
        carried[:share, :] = rows[pl.ds(start, share), :]
        carried[share:, :] = rows[n_dp * share :, :]


def widen(tokens, ids, weight, info, experts, share, n_dp):
    count, width = tokens.shape
    shapes = [jax.ShapeDtypeStruct((count, width + LANES), tokens.dtype)]
    if share:
        shapes.append(jax.ShapeDtypeStruct((count - (n_dp - 1) * share, width + LANES), tokens.dtype))

    def body(info_ref, tokens_ref, ids_ref, weight_ref, *outs):
        widen_body(experts, share, n_dp, info_ref, tokens_ref, ids_ref, weight_ref, outs[0], outs[1] if share else None)

    out = pl.pallas_call(
        body,
        out_shape=shapes,
        in_specs=[pl.BlockSpec(memory_space=pltpu.SMEM)] + [pl.BlockSpec(memory_space=pltpu.VMEM)] * 3,
        out_specs=[pl.BlockSpec(memory_space=pltpu.VMEM)] * len(shapes),
        compiler_params=pltpu.CompilerParams(vmem_limit_bytes=16 * 1024 * 1024),
        name="widen",
    )(info, tokens, ids, weight)
    return out[0], out[1] if share else out[0]


def ffn_body(layout, experts, blocks, out_rows, scaled, n_in, n_out, *refs):
    info = refs[0]
    inputs = refs[1 : 1 + n_in]
    gate, up, down = refs[1 + n_in : 4 + n_in]
    outs = refs[4 + n_in : 4 + n_in + n_out]
    x, gate_v, up_v, down_v, act, result, x_sem, gate_sem, up_sem, down_sem, out_sem = refs[4 + n_in + n_out :]
    width, hidden = gate.shape
    steps = hidden // TILE
    per_block = width // blocks // TILE
    dp = info[0]

    copies = []
    for number, (which, source, size, fixed, unit, flip) in enumerate(layout):
        start = fixed
        if unit:
            start = pl.multiple_of(fixed + (dp ^ flip) * unit, 16)
        copies.append(
            pltpu.make_async_copy(
                inputs[which].at[pl.ds(source, size), :], x.at[pl.ds(start, size), :], x_sem.at[number]
            )
        )

    def side(weights, held, sems, j):
        return pltpu.make_async_copy(
            weights.at[:, pl.ds(pl.multiple_of(j * TILE, TILE), TILE)], held.at[j], sems.at[j]
        )

    def lower(i):
        column = ((i // per_block) ^ dp if blocks > 1 else 0) * (width // blocks) + (i % per_block) * TILE
        return pltpu.make_async_copy(
            down.at[:, pl.ds(pl.multiple_of(column, TILE), TILE)], down_v.at[i], down_sem.at[i]
        )

    def leave(i):
        given = []
        for number, (first, count) in enumerate(out_rows):
            given.append(
                pltpu.make_async_copy(
                    result.at[i, pl.ds(first, count), :],
                    outs[number].at[i // per_block, :, pl.ds(pl.multiple_of((i % per_block) * TILE, TILE), TILE)],
                    out_sem.at[i, number],
                )
            )
        return given

    for copy in copies:
        copy.start()
    for j in range(steps):
        side(gate, gate_v, gate_sem, j).start()
        side(up, up_v, up_sem, j).start()
    for i in range(blocks * per_block):
        lower(i).start()
    for copy in copies:
        copy.wait()

    def first(j, carry):
        side(gate, gate_v, gate_sem, j).wait()
        side(up, up_v, up_sem, j).wait()
        rows = x[:, :width]
        gate_val = jnp.dot(rows, gate_v[j], preferred_element_type=jnp.float32)
        up_val = jnp.dot(rows, up_v[j], preferred_element_type=jnp.float32)
        value = gate_val / (1.0 + jnp.exp(-gate_val)) * up_val
        act[:, pl.ds(pl.multiple_of(j * TILE, TILE), TILE)] = value.astype(act.dtype)
        return carry

    lax.fori_loop(0, steps, first, 0)

    if scaled:
        held = x[:, width:].astype(jnp.float32)
        lane = lax.broadcasted_iota(jnp.int32, held.shape, 1)
        factor = jnp.sum(jnp.where(lane % experts == info[1], held, 0.0), axis=1, keepdims=True)

    def second(i, carry):
        lower(i).wait()
        value = jnp.dot(act[...], down_v[i], preferred_element_type=jnp.float32)
        if scaled:
            value = value * factor
        result[i] = value.astype(result.dtype)
        for copy in leave(i):
            copy.start()
        return carry

    lax.fori_loop(0, blocks * per_block, second, 0)

    def finish(i, carry):
        for copy in leave(i):
            copy.wait()
        return carry

    lax.fori_loop(0, blocks * per_block, finish, 0)


def ffn(info, inputs, layout, gate, up, down, experts, blocks, out_rows, scaled, dtype, name):
    width, hidden = gate.shape
    row_width = inputs[0].shape[1]
    rows = sum(count for _, count in out_rows)
    tiles = width // TILE
    steps = hidden // TILE
    flops = 6 * rows * width * hidden
    body = functools.partial(ffn_body, layout, experts, blocks, out_rows, scaled, len(inputs), len(out_rows))
    return pl.pallas_call(
        body,
        out_shape=[jax.ShapeDtypeStruct((blocks, count, width // blocks), dtype) for _, count in out_rows],
        in_specs=[pl.BlockSpec(memory_space=pltpu.SMEM)] + [pl.BlockSpec(memory_space=pl.ANY)] * (len(inputs) + 3),
        out_specs=[pl.BlockSpec(memory_space=pl.ANY)] * len(out_rows),
        scratch_shapes=[
            pltpu.VMEM((rows, row_width), jnp.bfloat16),
            pltpu.VMEM((steps, width, TILE), jnp.bfloat16),
            pltpu.VMEM((steps, width, TILE), jnp.bfloat16),
            pltpu.VMEM((tiles, hidden, TILE), jnp.bfloat16),
            pltpu.VMEM((rows, hidden), jnp.bfloat16),
            pltpu.VMEM((tiles, rows, TILE), dtype),
            pltpu.SemaphoreType.DMA((len(layout),)),
            pltpu.SemaphoreType.DMA((steps,)),
            pltpu.SemaphoreType.DMA((steps,)),
            pltpu.SemaphoreType.DMA((tiles,)),
            pltpu.SemaphoreType.DMA((tiles, len(out_rows))),
        ],
        compiler_params=pltpu.CompilerParams(vmem_limit_bytes=VMEM),
        cost_estimate=pl.CostEstimate(
            flops=flops, bytes_accessed=6 * width * hidden + 4 * rows * width, transcendentals=rows * hidden
        ),
        name=name,
    )(info, *inputs, gate, up, down)


def local(
    tokens,
    expert_ids,
    route_weight,
    pair_swap,
    expert_gate,
    expert_up,
    expert_down,
    shared_gate,
    shared_up,
    shared_down,
):
    count, width = tokens.shape
    experts = lax.axis_size("expert")
    n_dp = lax.axis_size("dp")
    half_axis = experts // 2
    column = lax.axis_index("expert")
    dp = lax.axis_index("dp")
    mine = jnp.where(pair_swap[column % half_axis] == 1, (column + half_axis) % experts, column)
    info = jnp.stack([dp, mine]).astype(jnp.int32)
    share = 3 * count // (4 * n_dp) // 16 * 16
    blocks = n_dp if (width // n_dp) % TILE == 0 else 1
    f32, bf16 = jnp.float32, jnp.bfloat16
    wide, carried = widen(tokens, expert_ids, route_weight, info, experts, share, n_dp)

    def by_dp(value):
        if blocks == n_dp:
            return value
        rows = value.shape[1]
        parts = value.reshape(rows, n_dp, width // n_dp)
        return jnp.take(parts, dp ^ jnp.arange(n_dp), axis=1).transpose(1, 0, 2)

    weights = (expert_gate[0], expert_up[0], expert_down[0])
    kept_rows = ((0, 2 * count), (2 * count, 2 * count))

    def gathered(distance):
        if distance == 0:
            across = exchange(wide, "expert", 2)
            inputs = [wide, across, exchange(wide, "expert", 1), exchange(across, "expert", 1)]
            layout = tuple((which, 0, count, which * count, 0, 0) for which in range(4))
            return inputs, layout
        mine_rows = exchange(carried, "expert", 4 * distance)
        across = exchange(mine_rows, "expert", 2)
        parts = [mine_rows, across]
        if share:
            both = jnp.concatenate([mine_rows[:share], across[:share]], axis=0)
            for flip in range(1, n_dp):
                parts.append(exchange(both, "dp", flip))
        own = jnp.concatenate(parts, axis=0)
        other = exchange(own, "expert", 1)
        held = carried.shape[0]
        layout = []
        for which in range(2):
            for shard in range(2):
                base = (2 * which + shard) * count
                at = shard * held
                if share:
                    layout.append((which, at, share, base, share, 0))
                if held > share:
                    layout.append((which, at + share, held - share, base + n_dp * share, 0, 0))
                for flip in range(1, n_dp if share else 1):
                    layout.append((which, 2 * held + (2 * flip - 2 + shard) * share, share, base, share, flip))
        return [own, other], tuple(layout)

    def spread(kept, sent, extra, across_first):
        kept, met = by_dp(kept), exchange(by_dp(sent), "expert", 1)
        if across_first:
            outer = (kept[:, count:].astype(f32) + met[:, count:].astype(f32)).astype(bf16)
            came = exchange(outer, "expert", 2)
            total = kept[:, :count].astype(f32) + met[:, :count].astype(f32) + came.astype(f32)
            if extra is not None:
                total = total + by_dp(extra)
            result = total[0]
            for flip in range(1, n_dp):
                result = result + exchange(total[flip].astype(bf16), "dp", flip).astype(f32)
            return result
        total = kept[0].astype(f32) + met[0].astype(f32)
        for flip in range(1, n_dp):
            outer = (kept[flip].astype(f32) + met[flip].astype(f32)).astype(bf16)
            total = total + exchange(outer, "dp", flip).astype(f32)
        came = exchange(total[count:].astype(bf16), "expert", 2)
        return total[:count] + came.astype(f32)

    shared_part = ffn(
        info,
        [tokens],
        ((0, 0, count, 0, 0, 0),),
        shared_gate,
        shared_up,
        shared_down,
        experts,
        blocks,
        ((0, count),),
        False,
        f32,
        "shared_expert",
    )[0]
    answer = None
    for distance in range(experts // 4):
        inputs, layout = gathered(distance)
        kept, sent = ffn(
            info, inputs, layout, *weights, experts, blocks, kept_rows, True, bf16, "routed_expert"
        )
        part = spread(kept, sent, shared_part if distance == 0 else None, distance % 2 == 0)
        if distance:
            part = exchange(part.astype(bf16), "expert", 4 * distance).astype(f32)
        answer = part if answer is None else answer + part
    return answer.astype(bf16)


def solution(mesh):
    in_specs = (
        P("expert", None),
        P("expert", None),
        P("expert", None),
        P(),
        P("expert", None, "dp"),
        P("expert", None, "dp"),
        P("expert", "dp", None),
        P(None, "dp"),
        P(None, "dp"),
        P("dp", None),
    )
    out_specs = P("expert", "dp")
    return jax.shard_map(local, mesh=mesh, in_specs=in_specs, out_specs=out_specs, check_vma=False)
```

```python
import functools

import jax
import jax.numpy as jnp
from jax import lax
from jax.experimental import pallas as pl
from jax.experimental.pallas import tpu as pltpu
from jax.sharding import PartitionSpec as P

routed_scale = 2.5
LANES = 128
SIDE = 256
AHEAD = 2
VMEM = 52 * 1024 * 1024


def exchange(value, axis, mask):
    pairs = [(source, source ^ mask) for source in range(lax.axis_size(axis))]
    return lax.ppermute(value, axis, pairs)


def widen_body(experts, tokens, ids, weight, rows):
    count, width = tokens.shape
    rates = weight[...]
    rates = routed_scale * rates / jnp.sum(rates, axis=1, keepdims=True)
    lane = lax.broadcasted_iota(jnp.int32, (count, LANES), 1)
    total = jnp.zeros((count, LANES), jnp.float32)
    for choice in range(ids.shape[1]):
        total += jnp.where(ids[:, choice : choice + 1] == lane % experts, rates[:, choice : choice + 1], 0.0)
    high = total.astype(jnp.bfloat16).astype(jnp.float32)
    middle = (total - high).astype(jnp.bfloat16).astype(jnp.float32)
    low = total - high - middle
    term = lane // experts
    held = jnp.where(term == 0, high, jnp.where(term == 1, middle, jnp.where(term == 2, low, 0.0)))
    rows[:, :width] = tokens[...]
    rows[:, width:] = held.astype(jnp.bfloat16)


def widen(tokens, ids, weight, experts):
    count, width = tokens.shape
    return pl.pallas_call(
        functools.partial(widen_body, experts),
        out_shape=jax.ShapeDtypeStruct((count, width + LANES), tokens.dtype),
        in_specs=[pl.BlockSpec(memory_space=pltpu.VMEM)] * 3,
        out_specs=pl.BlockSpec(memory_space=pltpu.VMEM),
        compiler_params=pltpu.CompilerParams(vmem_limit_bytes=16 * 1024 * 1024),
        name="widen",
    )(tokens, ids, weight)


def ffn_body(experts, blocks, out_rows, scaled, added, n_in, n_out, *refs):
    info = refs[0]
    inputs = refs[1 : 1 + n_in]
    gate, up, down = refs[1 + n_in : 4 + n_in]
    extra = refs[4 + n_in] if added else None
    refs = refs[4 + n_in + added :]
    outs = refs[:n_out]
    x, gate_v, up_v, down_v, act, factor, result, x_sem, gate_sem, up_sem, down_sem, out_sem = refs[n_out : n_out + 12]
    width, hidden = gate.shape
    steps = hidden // SIDE
    tile = result.shape[2]
    per_block = width // blocks // tile
    dp = info[0]

    copies = []
    for number, source in enumerate(inputs):
        size = source.shape[0]
        copies.append(pltpu.make_async_copy(source, x.at[pl.ds(number * size, size), :], x_sem.at[number]))
    if added:
        extra_v, extra_sem = refs[n_out + 12 :]
        count = extra.shape[1]
        more = pltpu.make_async_copy(extra, extra_v, extra_sem.at[0])

    def side(weights, held, sems, j):
        return pltpu.make_async_copy(
            weights.at[:, pl.ds(pl.multiple_of(j * SIDE, SIDE), SIDE)], held.at[j], sems.at[j]
        )

    def lower(i):
        column = ((i // per_block) ^ dp if blocks > 1 else 0) * (width // blocks) + (i % per_block) * tile
        return pltpu.make_async_copy(
            down.at[:, pl.ds(pl.multiple_of(column, LANES), tile)], down_v.at[i], down_sem.at[i]
        )

    def leave(i):
        given = []
        for number, (first, count) in enumerate(out_rows):
            given.append(
                pltpu.make_async_copy(
                    result.at[i, pl.ds(first, count), :],
                    outs[number].at[i // per_block, :, pl.ds(pl.multiple_of((i % per_block) * tile, LANES), tile)],
                    out_sem.at[i, number],
                )
            )
        return given

    for copy in copies:
        copy.start()
    for j in range(min(AHEAD, steps)):
        side(gate, gate_v, gate_sem, j).start()
        side(up, up_v, up_sem, j).start()
    for copy in copies:
        copy.wait()

    if scaled:
        held = x[:, width:].astype(jnp.float32)
        lane = lax.broadcasted_iota(jnp.int32, held.shape, 1)
        chosen = jnp.sum(jnp.where(lane % experts == info[1], held, 0.0), axis=1, keepdims=True)
        factor[...] = jnp.broadcast_to(chosen, factor.shape)

    def lowers():
        for i in range(blocks * per_block):
            lower(i).start()

    if steps <= AHEAD:
        lowers()
    if added:
        more.start()

    def first(j, carry):
        side(gate, gate_v, gate_sem, j).wait()
        side(up, up_v, up_sem, j).wait()

        @pl.when(j + AHEAD < steps)
        def _():
            side(gate, gate_v, gate_sem, j + AHEAD).start()
            side(up, up_v, up_sem, j + AHEAD).start()

        @pl.when(j + AHEAD == steps - 1)
        def _():
            lowers()

        rows = x[:, :width]
        gate_val = jnp.dot(rows, gate_v[j], preferred_element_type=jnp.float32)
        up_val = jnp.dot(rows, up_v[j], preferred_element_type=jnp.float32)
        value = gate_val / (1.0 + jnp.exp(-gate_val)) * up_val
        if scaled:
            value = value * factor[...]
        act[:, pl.ds(pl.multiple_of(j * SIDE, SIDE), SIDE)] = value.astype(act.dtype)
        return carry

    lax.fori_loop(0, steps, first, 0)

    if added:
        more.wait()

    def second(i, carry):
        lower(i).wait()
        value = jnp.dot(act[...], down_v[i], preferred_element_type=jnp.float32)
        if added:
            result[i, :count, :] = (value[:count] + extra_v[i]).astype(result.dtype)
            result[i, count:, :] = value[count:].astype(result.dtype)
        else:
            result[i] = value.astype(result.dtype)
        for copy in leave(i):
            copy.start()
        return carry

    lax.fori_loop(0, blocks * per_block, second, 0)

    def finish(i, carry):
        for copy in leave(i):
            copy.wait()
        return carry

    lax.fori_loop(0, blocks * per_block, finish, 0)


def ffn(info, inputs, gate, up, down, extra, experts, blocks, out_rows, scaled, dtype, name):
    width, hidden = gate.shape
    row_width = inputs[0].shape[1]
    rows = sum(count for _, count in out_rows)
    tiles = max(blocks, 2)
    tile = width // tiles
    steps = hidden // SIDE
    flops = 6 * rows * width * hidden
    added = 0 if extra is None else 1
    body = functools.partial(ffn_body, experts, blocks, out_rows, scaled, added, len(inputs), len(out_rows))
    scratch = [
        pltpu.VMEM((rows, row_width), jnp.bfloat16),
        pltpu.VMEM((steps, width, SIDE), jnp.bfloat16),
        pltpu.VMEM((steps, width, SIDE), jnp.bfloat16),
        pltpu.VMEM((tiles, hidden, tile), jnp.bfloat16),
        pltpu.VMEM((rows, hidden), jnp.bfloat16),
        pltpu.VMEM((rows, SIDE), jnp.float32),
        pltpu.VMEM((tiles, rows, tile), dtype),
        pltpu.SemaphoreType.DMA((len(inputs),)),
        pltpu.SemaphoreType.DMA((steps,)),
        pltpu.SemaphoreType.DMA((steps,)),
        pltpu.SemaphoreType.DMA((tiles,)),
        pltpu.SemaphoreType.DMA((tiles, len(out_rows))),
    ]
    if added:
        scratch += [pltpu.VMEM((tiles, extra.shape[1], tile), jnp.float32), pltpu.SemaphoreType.DMA((1,))]
    return pl.pallas_call(
        body,
        out_shape=[jax.ShapeDtypeStruct((blocks, count, width // blocks), dtype) for _, count in out_rows],
        in_specs=[pl.BlockSpec(memory_space=pltpu.SMEM)]
        + [pl.BlockSpec(memory_space=pltpu.HBM)] * (len(inputs) + 3 + added),
        out_specs=[pl.BlockSpec(memory_space=pltpu.HBM)] * len(out_rows),
        scratch_shapes=scratch,
        compiler_params=pltpu.CompilerParams(vmem_limit_bytes=VMEM),
        cost_estimate=pl.CostEstimate(
            flops=flops, bytes_accessed=6 * width * hidden + 4 * rows * width, transcendentals=rows * hidden
        ),
        name=name,
    )(info, *inputs, gate, up, down, *([extra] if added else []))


def local(
    tokens,
    expert_ids,
    route_weight,
    pair_swap,
    expert_gate,
    expert_up,
    expert_down,
    shared_gate,
    shared_up,
    shared_down,
):
    count, width = tokens.shape
    experts = lax.axis_size("expert")
    n_dp = lax.axis_size("dp")
    half_axis = experts // 2
    column = lax.axis_index("expert")
    dp = lax.axis_index("dp")
    mine = jnp.where(pair_swap[column % half_axis] == 1, (column + half_axis) % experts, column)
    info = jnp.stack([dp, mine]).astype(jnp.int32)
    blocks = n_dp if (width // n_dp) % LANES == 0 else 1
    planes = experts // 4
    plane = column // 4
    f32, bf16 = jnp.float32, jnp.bfloat16
    weights = (expert_gate[0], expert_up[0], expert_down[0])
    def over_core(value):
        return exchange(value, "expert", 1)

    def over_row(value):
        return exchange(value, "expert", 2)

    def over_dp(sends):
        return [exchange(send, "dp", k + 1) for k, send in enumerate(sends)]

    def over_planes(value, pairs):
        return lax.ppermute(value, "expert", [(4 * s + k, 4 * t + k) for s, t in pairs for k in range(4)])

    def by_dp(value):
        if blocks == n_dp:
            return value
        rows = value.shape[1]
        parts = value.transpose(1, 0, 2).reshape(rows, n_dp, width // n_dp)
        return jnp.take(parts, dp ^ jnp.arange(n_dp), axis=1).transpose(1, 0, 2)

    def routed(inputs, extra=None):
        half = len(inputs) // 2 * count
        halves = ((0, half), (half, half))
        kept, sent = ffn(info, inputs, *weights, extra, experts, blocks, halves, True, bf16, "routed_expert")
        return by_dp(kept), by_dp(sent)

    def to_dp(kept, met):
        return [(kept[k].astype(f32) + met[k].astype(f32)).astype(bf16) for k in range(1, n_dp)]

    def owned(kept, met, came):
        whole = kept[0].astype(f32) + met[0].astype(f32)
        for value in came:
            whole = whole + value.astype(f32)
        return whole

    def together(*values):
        return lax.optimization_barrier(values)

    wide = widen(tokens, expert_ids, route_weight, experts)
    shared_part = ffn(
        info,
        [tokens],
        shared_gate,
        shared_up,
        shared_down,
        None,
        experts,
        blocks,
        ((0, count),),
        False,
        f32,
        "shared_expert",
    )[0]
    if blocks == 1:
        shared_part = shared_part.reshape(count, 2, width // 2).transpose(1, 0, 2)

    if planes == 4:
        inner = (plane == 1) | (plane == 2)
        middle, outward = ((1, 2), (2, 1)), ((1, 0), (2, 3))
        row_own = over_row(wide)
        near = over_planes(wide, ((0, 1), (1, 0), (2, 3), (3, 2)))
        opposite = over_planes(wide, middle)
        kept_0, sent_0 = routed([wide, over_core(wide)], shared_part)
        kept_0, sent_0, row_own, near, opposite = together(kept_0, sent_0, row_own, near, opposite)

        inputs = [row_own, near, over_core(row_own), over_core(near)]
        row_near = over_row(near)
        from_outer, from_inner = over_planes(opposite, outward), over_planes(near, middle)
        met_0 = over_core(sent_0)
        came_0 = over_dp(to_dp(kept_0, met_0))
        kept_1, sent_1 = routed(inputs)
        kept_1, sent_1, row_near, from_outer, from_inner, *came_0 = together(
            kept_1, sent_1, row_near, from_outer, from_inner, *came_0
        )

        next_ = jnp.where(inner, from_inner, from_outer)
        inputs = [row_near, next_, over_core(row_near), over_core(next_)]
        row_next = over_row(next_)
        last = over_planes(from_inner, outward)
        met_1 = over_core(sent_1)
        came_1 = over_dp(to_dp(kept_1, met_1))
        kept_2, sent_2 = routed(inputs)
        kept_2, sent_2, row_next, last, *came_1 = together(kept_2, sent_2, row_next, last, *came_1)

        far = jnp.where(inner, opposite, last)
        inputs = [row_next, far, over_core(row_next), over_core(far)]
        row_far = over_row(far)
        met_2 = over_core(sent_2)
        whole_1 = owned(kept_1, met_1, came_1)
        back_0 = over_row(whole_1[:count].astype(bf16))
        came_2 = over_dp(to_dp(kept_2, met_2))
        kept_3, sent_3 = routed(inputs)
        kept_3, sent_3, row_far, back_0, *came_2 = together(kept_3, sent_3, row_far, back_0, *came_2)

        inputs = [row_far, over_core(row_far)]
        met_3 = over_core(sent_3)
        whole_2 = owned(kept_2, met_2, came_2)
        back_1 = over_row(whole_2[:count].astype(bf16))
        came_3 = over_dp(to_dp(kept_3, met_3))
        kept_4, sent_4 = routed(inputs)
        kept_4, sent_4, back_1, *came_3 = together(kept_4, sent_4, back_1, *came_3)

        met_4 = over_core(sent_4)
        whole_3 = owned(kept_3, met_3, came_3)
        back_2 = over_row(whole_3[:count].astype(bf16))
        came_4 = over_dp(to_dp(kept_4, met_4))
        back_3 = over_row(owned(kept_4, met_4, came_4).astype(bf16))
        totals = [
            owned(kept_0, met_0, came_0) + back_0.astype(f32),
            whole_1[count:] + back_1.astype(f32),
            whole_2[count:] + back_2.astype(f32),
            whole_3[count:] + back_3.astype(f32),
        ]
    else:
        totals = []
        for s in range(planes):
            here = exchange(wide, "expert", 4 * s) if s else wide
            across = over_row(here)
            kept, sent = routed([here, across, over_core(here), over_core(across)], None if s else shared_part)
            met = over_core(sent)
            whole = owned(kept, met, over_dp(to_dp(kept, met)))
            totals.append(whole[:count] + over_row(whole[count:].astype(bf16)).astype(f32))
    answer = totals[0]
    for s in range(1, planes):
        answer = answer + exchange(totals[s].astype(bf16), "expert", 4 * s).astype(f32)
    return answer.astype(bf16)


def solution(mesh):
    in_specs = (
        P("expert", None),
        P("expert", None),
        P("expert", None),
        P(),
        P("expert", None, "dp"),
        P("expert", None, "dp"),
        P("expert", "dp", None),
        P(None, "dp"),
        P(None, "dp"),
        P("dp", None),
    )
    out_specs = P("expert", "dp")
    return jax.shard_map(local, mesh=mesh, in_specs=in_specs, out_specs=out_specs, check_vma=False)
```

```python
import functools

import jax
import jax.numpy as jnp
from jax import lax
from jax.experimental import pallas as pl
from jax.experimental.pallas import tpu as pltpu
from jax.sharding import PartitionSpec as P

routed_scale = 2.5
LANES = 128
SIDE = 256
AHEAD = 2
VMEM = 42 * 1024 * 1024


def exchange(value, axis, mask):
    pairs = [(source, source ^ mask) for source in range(lax.axis_size(axis))]
    return lax.ppermute(value, axis, pairs)


def widen_body(experts, tokens, ids, weight, rows):
    count, width = tokens.shape
    ids = jnp.transpose(ids[...])
    rates = jnp.transpose(weight[...])
    rates = routed_scale * rates / jnp.sum(rates, axis=1, keepdims=True)
    lane = lax.broadcasted_iota(jnp.int32, (count, LANES), 1)
    total = jnp.zeros((count, LANES), jnp.float32)
    for choice in range(ids.shape[1]):
        total += jnp.where(ids[:, choice : choice + 1] == lane % experts, rates[:, choice : choice + 1], 0.0)
    high = total.astype(jnp.bfloat16).astype(jnp.float32)
    middle = (total - high).astype(jnp.bfloat16).astype(jnp.float32)
    low = total - high - middle
    term = lane // experts
    held = jnp.where(term == 0, high, jnp.where(term == 1, middle, jnp.where(term == 2, low, 0.0)))
    rows[:, :width] = tokens[...]
    rows[:, width:] = held.astype(jnp.bfloat16)


def widen(tokens, ids, weight, experts):
    count, width = tokens.shape
    return pl.pallas_call(
        functools.partial(widen_body, experts),
        out_shape=jax.ShapeDtypeStruct((count, width + LANES), tokens.dtype),
        grid=(1,),
        in_specs=[pl.BlockSpec(array.shape, lambda i: (0, 0)) for array in (tokens, ids.T, weight.T)],
        out_specs=pl.BlockSpec((count, width + LANES), lambda i: (0, 0)),
        compiler_params=pltpu.CompilerParams(vmem_limit_bytes=16 * 1024 * 1024),
        name="widen",
    )(tokens, ids.T, weight.T)


def ffn_body(experts, blocks, out_rows, scaled, n_in, n_out, *refs):
    info = refs[0]
    inputs = refs[1 : 1 + n_in]
    gate, up, down = refs[1 + n_in : 4 + n_in]
    refs = refs[4 + n_in :]
    outs = refs[:n_out]
    x, gate_v, up_v, down_v, act, factor, result, x_sem, gate_sem, up_sem, down_sem, out_sem = refs[n_out:]
    width, hidden = gate.shape
    steps = hidden // SIDE
    tile = result.shape[2]
    per_block = width // blocks // tile
    dp = info[0]

    copies = []
    for number, source in enumerate(inputs):
        size = source.shape[0]
        copies.append(pltpu.make_async_copy(source, x.at[pl.ds(number * size, size), :], x_sem.at[number]))
    def side(weights, held, sems, j):
        return pltpu.make_async_copy(
            weights.at[:, pl.ds(pl.multiple_of(j * SIDE, SIDE), SIDE)], held.at[j], sems.at[j]
        )

    def lower(i):
        column = ((i // per_block) ^ dp if blocks > 1 else 0) * (width // blocks) + (i % per_block) * tile
        return pltpu.make_async_copy(
            down.at[:, pl.ds(pl.multiple_of(column, LANES), tile)], down_v.at[i], down_sem.at[i]
        )

    def leave(i):
        given = []
        for number, (first, count) in enumerate(out_rows):
            given.append(
                pltpu.make_async_copy(
                    result.at[i, pl.ds(first, count), :],
                    outs[number].at[i // per_block, :, pl.ds(pl.multiple_of((i % per_block) * tile, LANES), tile)],
                    out_sem.at[i, number],
                )
            )
        return given

    for copy in copies:
        copy.start()
    for j in range(min(AHEAD, steps)):
        side(gate, gate_v, gate_sem, j).start()
        side(up, up_v, up_sem, j).start()
    for copy in copies:
        copy.wait()

    if scaled:
        held = x[:, width:].astype(jnp.float32)
        lane = lax.broadcasted_iota(jnp.int32, held.shape, 1)
        chosen = jnp.sum(jnp.where(lane % experts == info[1], held, 0.0), axis=1, keepdims=True)
        factor[...] = jnp.broadcast_to(chosen, factor.shape)

    def lowers():
        for i in range(blocks * per_block):
            lower(i).start()

    if steps <= AHEAD:
        lowers()

    def first(j, carry):
        side(gate, gate_v, gate_sem, j).wait()
        side(up, up_v, up_sem, j).wait()

        @pl.when(j + AHEAD < steps)
        def _():
            side(gate, gate_v, gate_sem, j + AHEAD).start()
            side(up, up_v, up_sem, j + AHEAD).start()

        @pl.when(j + AHEAD == steps - 1)
        def _():
            lowers()

        rows = x[:, :width]
        gate_val = jnp.dot(rows, gate_v[j], preferred_element_type=jnp.float32)
        up_val = jnp.dot(rows, up_v[j], preferred_element_type=jnp.float32)
        value = gate_val / (1.0 + jnp.exp(-gate_val)) * up_val
        if scaled:
            value = value * factor[...]
        act[:, pl.ds(pl.multiple_of(j * SIDE, SIDE), SIDE)] = value.astype(act.dtype)
        return carry

    lax.fori_loop(0, steps, first, 0)

    def second(i, carry):
        lower(i).wait()
        value = jnp.dot(act[...], down_v[i], preferred_element_type=jnp.float32)
        result[i] = value.astype(result.dtype)
        for copy in leave(i):
            copy.start()
        return carry

    lax.fori_loop(0, blocks * per_block, second, 0)

    def finish(i, carry):
        for copy in leave(i):
            copy.wait()
        return carry

    lax.fori_loop(0, blocks * per_block, finish, 0)


def ffn(info, inputs, gate, up, down, experts, blocks, out_rows, scaled, dtype, name):
    width, hidden = gate.shape
    row_width = inputs[0].shape[1]
    rows = sum(count for _, count in out_rows)
    tiles = max(blocks, 2)
    tile = width // tiles
    steps = hidden // SIDE
    flops = 6 * rows * width * hidden
    body = functools.partial(ffn_body, experts, blocks, out_rows, scaled, len(inputs), len(out_rows))
    scratch = [
        pltpu.VMEM((rows, row_width), jnp.bfloat16),
        pltpu.VMEM((steps, width, SIDE), jnp.bfloat16),
        pltpu.VMEM((steps, width, SIDE), jnp.bfloat16),
        pltpu.VMEM((tiles, hidden, tile), jnp.bfloat16),
        pltpu.VMEM((rows, hidden), jnp.bfloat16),
        pltpu.VMEM((rows, SIDE), jnp.float32),
        pltpu.VMEM((tiles, rows, tile), dtype),
        pltpu.SemaphoreType.DMA((len(inputs),)),
        pltpu.SemaphoreType.DMA((steps,)),
        pltpu.SemaphoreType.DMA((steps,)),
        pltpu.SemaphoreType.DMA((tiles,)),
        pltpu.SemaphoreType.DMA((tiles, len(out_rows))),
    ]
    return pl.pallas_call(
        body,
        out_shape=[jax.ShapeDtypeStruct((blocks, count, width // blocks), dtype) for _, count in out_rows],
        in_specs=[pl.BlockSpec(memory_space=pltpu.SMEM)]
        + [pl.BlockSpec(memory_space=pl.ANY)] * (len(inputs) + 3),
        out_specs=[pl.BlockSpec(memory_space=pl.ANY)] * len(out_rows),
        scratch_shapes=scratch,
        compiler_params=pltpu.CompilerParams(vmem_limit_bytes=VMEM),
        cost_estimate=pl.CostEstimate(
            flops=flops, bytes_accessed=6 * width * hidden + 4 * rows * width, transcendentals=rows * hidden
        ),
        name=name,
    )(info, *inputs, *[pltpu.with_memory_space_constraint(array, pltpu.HBM) for array in (gate, up, down)])


def local(
    tokens,
    expert_ids,
    route_weight,
    pair_swap,
    expert_gate,
    expert_up,
    expert_down,
    shared_gate,
    shared_up,
    shared_down,
):
    count, width = tokens.shape
    experts = lax.axis_size("expert")
    n_dp = lax.axis_size("dp")
    half_axis = experts // 2
    column = lax.axis_index("expert")
    dp = lax.axis_index("dp")
    mine = jnp.where(pair_swap[column % half_axis] == 1, (column + half_axis) % experts, column)
    info = jnp.stack([dp, mine]).astype(jnp.int32)
    blocks = n_dp if (width // n_dp) % LANES == 0 else 1
    planes = experts // 4
    plane = column // 4
    f32, bf16 = jnp.float32, jnp.bfloat16
    weights = (expert_gate[0], expert_up[0], expert_down[0])
    def over_core(value):
        return exchange(value, "expert", 1)

    def over_row(value):
        return exchange(value, "expert", 2)

    def over_dp(sends):
        return [exchange(send, "dp", k + 1) for k, send in enumerate(sends)]

    def across_both(value, k):
        pairs = [(d * experts + e, (d ^ k) * experts + (e ^ 2)) for d in range(n_dp) for e in range(experts)]
        return lax.ppermute(value, ("dp", "expert"), pairs)

    def over_planes(value, pairs):
        return lax.ppermute(value, "expert", [(4 * s + k, 4 * t + k) for s, t in pairs for k in range(4)])

    def by_dp(value):
        if blocks == n_dp:
            return value
        rows = value.shape[1]
        parts = value.transpose(1, 0, 2).reshape(rows, n_dp, width // n_dp)
        return jnp.take(parts, dp ^ jnp.arange(n_dp), axis=1).transpose(1, 0, 2)

    def routed(inputs):
        half = len(inputs) // 2 * count
        halves = ((0, half), (half, half))
        kept, sent = ffn(info, inputs, *weights, experts, blocks, halves, True, bf16, "routed_expert")
        return by_dp(kept), by_dp(sent)

    def shared(rows):
        halves = ((0, count),)
        out = ffn(info, [rows], shared_gate, shared_up, shared_down, experts, blocks, halves, False, f32, "shared_expert")
        return by_dp(out[0])

    def to_dp(kept, met, part=slice(None)):
        return [(kept[k, part].astype(f32) + met[k, part].astype(f32)).astype(bf16) for k in range(1, n_dp)]

    def owned(kept, met, came, part=slice(None)):
        whole = kept[0, part].astype(f32) + met[0, part].astype(f32)
        for value in came:
            whole = whole + value.astype(f32)
        return whole

    def of(values, part):
        return [value[part] for value in values]

    def together(*values):
        return lax.optimization_barrier(values)

    upper, lower = slice(None, count), slice(count, None)
    wide = widen(tokens, expert_ids, route_weight, experts)
    if planes == 4:
        inner = (plane == 1) | (plane == 2)
        cut = count * 3 // 4
        middle, outward = ((1, 2), (2, 1)), ((1, 0), (2, 3))
        row_own = over_row(wide)
        near = over_planes(wide, ((0, 1), (1, 0), (2, 3), (3, 2)))
        opposite = over_planes(wide, middle)
        shared_part = shared(tokens)
        kept_0, sent_0 = routed([wide, over_core(wide)])
        kept_0, near, opposite = together(kept_0, near, opposite)
        kept_0, sent_0, row_own, shared_part = together(kept_0, sent_0, row_own, shared_part)

        inputs = [row_own, near, over_core(row_own), over_core(near)]
        row_near = over_row(near)
        from_outer, from_inner = over_planes(opposite, outward), over_planes(near, middle)
        met_0 = over_core(sent_0)
        own = kept_0.astype(f32) + met_0.astype(f32) + shared_part
        came_0 = over_dp([own[k].astype(bf16) for k in range(1, n_dp)])
        kept_1, sent_1 = routed(inputs)
        kept_1, sent_1, row_near, *came_0 = together(kept_1, sent_1, row_near, *came_0)
        kept_1, from_outer, from_inner = together(kept_1, from_outer, from_inner)

        next_ = jnp.where(inner, from_inner, from_outer)
        inputs = [row_near, next_, over_core(row_near), over_core(next_)]
        row_next = over_row(next_)
        last = over_planes(from_inner, outward)
        met_1 = over_core(sent_1)
        came_1 = over_dp(to_dp(kept_1, met_1))
        kept_2, sent_2 = routed(inputs)
        kept_2, sent_2, row_next, *came_1 = together(kept_2, sent_2, row_next, *came_1)
        kept_2, last = together(kept_2, last)

        far = jnp.where(inner, opposite, last)
        inputs = [row_next, far, over_core(row_next), over_core(far)]
        row_far = over_row(far)
        met_2 = over_core(sent_2)
        home_1 = exchange(owned(kept_1, met_1, of(came_1, lower), lower).astype(bf16), "expert", 4)
        came_2 = over_dp(to_dp(kept_2, met_2))
        kept_3, sent_3 = routed(inputs)
        kept_3, sent_3, row_far, home_1, *came_2 = together(kept_3, sent_3, row_far, home_1, *came_2)

        inputs = [row_far, over_core(row_far)]
        met_3 = over_core(sent_3)
        cross_1 = exchange(owned(kept_2, met_2, of(came_2, upper), upper).astype(bf16), "expert", 4)
        total_2 = owned(kept_2, met_2, of(came_2, lower), lower).astype(bf16)
        home_2 = exchange(total_2[:cut], "expert", 8)
        came_3 = over_dp(to_dp(kept_3, met_3, upper))
        kept_4, sent_4 = routed(inputs)
        kept_4, sent_4, home_2, *came_3 = together(kept_4, sent_4, home_2, *came_3)

        met_4 = over_core(sent_4)
        sends = [(kept_4[k].astype(f32) + met_4[k].astype(f32)).astype(bf16) for k in range(n_dp)]
        back_3 = [over_row(sends[0])] + [across_both(send, k) for k, send in enumerate(sends) if k]
        cross_2 = owned(kept_3, met_3, came_3, upper).astype(bf16)
        cross_2 = exchange(jnp.concatenate([cross_2, total_2[cut:]], axis=0), "expert", 8)
        *sends, _ = together(*to_dp(kept_3, met_3, lower), sends[0])
        came_far = over_dp(sends)
        back_3[0], back_3[1], cross_1, cross_2, *came_far = together(*back_3[:2], cross_1, cross_2, *came_far)
        total_3 = owned(kept_3, met_3, came_far + back_3, lower)
        home_3 = exchange(total_3.astype(bf16), "expert", 12)
        cross = cross_1.astype(f32) + cross_2[:count].astype(f32)
        back_0 = over_row((owned(kept_1, met_1, of(came_1, upper), upper) + cross).astype(bf16))
        home_2 = jnp.concatenate([home_2, cross_2[count:]], axis=0)
        homes = [home_1, home_2, home_3]
        answer = own[0] + back_0.astype(f32)
        for value in came_0:
            answer = answer + value.astype(f32)
    else:
        totals = []
        for s in range(planes):
            here = exchange(wide, "expert", 4 * s) if s else wide
            across = over_row(here)
            kept, sent = routed([here, across, over_core(here), over_core(across)])
            met = over_core(sent)
            whole = owned(kept, met, over_dp(to_dp(kept, met)))
            totals.append(whole[:count] + over_row(whole[count:].astype(bf16)).astype(f32))
        homes = [exchange(totals[s].astype(bf16), "expert", 4 * s) for s in range(1, planes)]
        shared_part = shared(tokens)
        answer = totals[0] + shared_part[0]
        for value in over_dp([shared_part[k].astype(bf16) for k in range(1, n_dp)]):
            answer = answer + value.astype(f32)
    for value in homes:
        answer = answer + value.astype(f32)
    return answer.astype(bf16)


def solution(mesh):
    in_specs = (
        P("expert", None),
        P("expert", None),
        P("expert", None),
        P(),
        P("expert", None, "dp"),
        P("expert", None, "dp"),
        P("expert", "dp", None),
        P(None, "dp"),
        P(None, "dp"),
        P("dp", None),
    )
    out_specs = P("expert", "dp")
    return jax.shard_map(local, mesh=mesh, in_specs=in_specs, out_specs=out_specs, check_vma=False)
```

```python
import functools

import jax
import jax.numpy as jnp
from jax import lax
from jax.experimental import pallas as pl
from jax.experimental.pallas import tpu as pltpu
from jax.sharding import PartitionSpec as P

routed_scale = 2.5
LANES = 128
SIDE = 256
AHEAD = 2
VMEM = 42 * 1024 * 1024


def exchange(value, axis, mask):
    pairs = [(source, source ^ mask) for source in range(lax.axis_size(axis))]
    return lax.ppermute(value, axis, pairs)


def widen_body(experts, tokens, ids, weight, rows):
    count, width = tokens.shape
    ids = jnp.transpose(ids[...])
    rates = jnp.transpose(weight[...])
    rates = routed_scale * rates / jnp.sum(rates, axis=1, keepdims=True)
    lane = lax.broadcasted_iota(jnp.int32, (count, LANES), 1)
    total = jnp.zeros((count, LANES), jnp.float32)
    for choice in range(ids.shape[1]):
        total += jnp.where(ids[:, choice : choice + 1] == lane % experts, rates[:, choice : choice + 1], 0.0)
    high = total.astype(jnp.bfloat16).astype(jnp.float32)
    middle = (total - high).astype(jnp.bfloat16).astype(jnp.float32)
    low = total - high - middle
    term = lane // experts
    held = jnp.where(term == 0, high, jnp.where(term == 1, middle, jnp.where(term == 2, low, 0.0)))
    rows[:, :width] = tokens[...]
    rows[:, width:] = held.astype(jnp.bfloat16)


def widen(tokens, ids, weight, experts):
    count, width = tokens.shape
    return pl.pallas_call(
        functools.partial(widen_body, experts),
        out_shape=jax.ShapeDtypeStruct((count, width + LANES), tokens.dtype),
        grid=(1,),
        in_specs=[pl.BlockSpec(array.shape, lambda i: (0, 0)) for array in (tokens, ids.T, weight.T)],
        out_specs=pl.BlockSpec((count, width + LANES), lambda i: (0, 0)),
        compiler_params=pltpu.CompilerParams(vmem_limit_bytes=16 * 1024 * 1024),
        name="widen",
    )(tokens, ids.T, weight.T)


def ffn_body(experts, blocks, out_rows, scaled, n_in, n_out, *refs):
    info = refs[0]
    inputs = refs[1 : 1 + n_in]
    gate, up, down = refs[1 + n_in : 4 + n_in]
    refs = refs[4 + n_in :]
    outs = refs[:n_out]
    x, gate_v, up_v, down_v, act, factor, result, x_sem, gate_sem, up_sem, down_sem, out_sem = refs[n_out:]
    width, hidden = gate.shape
    steps = hidden // SIDE
    tile = result.shape[2]
    per_block = width // blocks // tile
    dp = info[0]

    copies = []
    for number, source in enumerate(inputs):
        size = source.shape[0]
        copies.append(pltpu.make_async_copy(source, x.at[pl.ds(number * size, size), :], x_sem.at[number]))
    def side(weights, held, sems, j):
        return pltpu.make_async_copy(
            weights.at[:, pl.ds(pl.multiple_of(j * SIDE, SIDE), SIDE)], held.at[j], sems.at[j]
        )

    def lower(i):
        column = ((i // per_block) ^ dp if blocks > 1 else 0) * (width // blocks) + (i % per_block) * tile
        return pltpu.make_async_copy(
            down.at[:, pl.ds(pl.multiple_of(column, LANES), tile)], down_v.at[i], down_sem.at[i]
        )

    def leave(i):
        given = []
        for number, (first, count) in enumerate(out_rows):
            given.append(
                pltpu.make_async_copy(
                    result.at[i, pl.ds(first, count), :],
                    outs[number].at[i // per_block, :, pl.ds(pl.multiple_of((i % per_block) * tile, LANES), tile)],
                    out_sem.at[i, number],
                )
            )
        return given

    for copy in copies:
        copy.start()
    for j in range(min(AHEAD, steps)):
        side(gate, gate_v, gate_sem, j).start()
        side(up, up_v, up_sem, j).start()
    for copy in copies:
        copy.wait()

    if scaled:
        held = x[:, width:].astype(jnp.float32)
        lane = lax.broadcasted_iota(jnp.int32, held.shape, 1)
        chosen = jnp.sum(jnp.where(lane % experts == info[1], held, 0.0), axis=1, keepdims=True)
        factor[...] = jnp.broadcast_to(chosen, factor.shape)

    def lowers():
        for i in range(blocks * per_block):
            lower(i).start()

    if steps <= AHEAD:
        lowers()

    def first(j, carry):
        side(gate, gate_v, gate_sem, j).wait()
        side(up, up_v, up_sem, j).wait()

        @pl.when(j + AHEAD < steps)
        def _():
            side(gate, gate_v, gate_sem, j + AHEAD).start()
            side(up, up_v, up_sem, j + AHEAD).start()

        @pl.when(j + AHEAD == steps - 1)
        def _():
            lowers()

        rows = x[:, :width]
        gate_val = jnp.dot(rows, gate_v[j], preferred_element_type=jnp.float32)
        up_val = jnp.dot(rows, up_v[j], preferred_element_type=jnp.float32)
        value = gate_val / (1.0 + jnp.exp(-gate_val)) * up_val
        if scaled:
            value = value * factor[...]
        act[:, pl.ds(pl.multiple_of(j * SIDE, SIDE), SIDE)] = value.astype(act.dtype)
        return carry

    lax.fori_loop(0, steps, first, 0)

    def second(i, carry):
        lower(i).wait()
        value = jnp.dot(act[...], down_v[i], preferred_element_type=jnp.float32)
        result[i] = value.astype(result.dtype)
        for copy in leave(i):
            copy.start()
        return carry

    lax.fori_loop(0, blocks * per_block, second, 0)

    def finish(i, carry):
        for copy in leave(i):
            copy.wait()
        return carry

    lax.fori_loop(0, blocks * per_block, finish, 0)


def ffn(info, inputs, gate, up, down, experts, blocks, out_rows, scaled, dtype, name):
    width, hidden = gate.shape
    row_width = inputs[0].shape[1]
    rows = sum(count for _, count in out_rows)
    tiles = max(blocks, 2)
    tile = width // tiles
    steps = hidden // SIDE
    flops = 6 * rows * width * hidden
    body = functools.partial(ffn_body, experts, blocks, out_rows, scaled, len(inputs), len(out_rows))
    scratch = [
        pltpu.VMEM((rows, row_width), jnp.bfloat16),
        pltpu.VMEM((steps, width, SIDE), jnp.bfloat16),
        pltpu.VMEM((steps, width, SIDE), jnp.bfloat16),
        pltpu.VMEM((tiles, hidden, tile), jnp.bfloat16),
        pltpu.VMEM((rows, hidden), jnp.bfloat16),
        pltpu.VMEM((rows, SIDE), jnp.float32),
        pltpu.VMEM((tiles, rows, tile), dtype),
        pltpu.SemaphoreType.DMA((len(inputs),)),
        pltpu.SemaphoreType.DMA((steps,)),
        pltpu.SemaphoreType.DMA((steps,)),
        pltpu.SemaphoreType.DMA((tiles,)),
        pltpu.SemaphoreType.DMA((tiles, len(out_rows))),
    ]
    return pl.pallas_call(
        body,
        out_shape=[jax.ShapeDtypeStruct((blocks, count, width // blocks), dtype) for _, count in out_rows],
        in_specs=[pl.BlockSpec(memory_space=pltpu.SMEM)]
        + [pl.BlockSpec(memory_space=pl.ANY)] * (len(inputs) + 3),
        out_specs=[pl.BlockSpec(memory_space=pl.ANY)] * len(out_rows),
        scratch_shapes=scratch,
        compiler_params=pltpu.CompilerParams(vmem_limit_bytes=VMEM),
        cost_estimate=pl.CostEstimate(
            flops=flops, bytes_accessed=6 * width * hidden + 4 * rows * width, transcendentals=rows * hidden
        ),
        name=name,
    )(info, *inputs, *[pltpu.with_memory_space_constraint(array, pltpu.HBM) for array in (gate, up, down)])


def local(
    tokens,
    expert_ids,
    route_weight,
    pair_swap,
    expert_gate,
    expert_up,
    expert_down,
    shared_gate,
    shared_up,
    shared_down,
):
    count, width = tokens.shape
    experts = lax.axis_size("expert")
    n_dp = lax.axis_size("dp")
    half_axis = experts // 2
    column = lax.axis_index("expert")
    dp = lax.axis_index("dp")
    mine = jnp.where(pair_swap[column % half_axis] == 1, (column + half_axis) % experts, column)
    info = jnp.stack([dp, mine]).astype(jnp.int32)
    blocks = n_dp if (width // n_dp) % LANES == 0 else 1
    planes = experts // 4
    plane = column // 4
    f32, bf16 = jnp.float32, jnp.bfloat16
    weights = (expert_gate[0], expert_up[0], expert_down[0])
    def over_core(value):
        return exchange(value, "expert", 1)

    def over_row(value):
        return exchange(value, "expert", 2)

    def over_dp(sends):
        return [exchange(send, "dp", k + 1) for k, send in enumerate(sends)]

    def across_both(value, k):
        pairs = [(d * experts + e, (d ^ k) * experts + (e ^ 2)) for d in range(n_dp) for e in range(experts)]
        return lax.ppermute(value, ("dp", "expert"), pairs)

    def over_planes(value, pairs):
        return lax.ppermute(value, "expert", [(4 * s + k, 4 * t + k) for s, t in pairs for k in range(4)])

    def by_dp(value):
        if blocks == n_dp:
            return value
        rows = value.shape[1]
        parts = value.transpose(1, 0, 2).reshape(rows, n_dp, width // n_dp)
        return jnp.take(parts, dp ^ jnp.arange(n_dp), axis=1).transpose(1, 0, 2)

    def routed(inputs):
        half = len(inputs) // 2 * count
        halves = ((0, half), (half, half))
        kept, sent = ffn(info, inputs, *weights, experts, blocks, halves, True, bf16, "routed_expert")
        return by_dp(kept), by_dp(sent)

    def shared(rows):
        halves = ((0, count),)
        out = ffn(info, [rows], shared_gate, shared_up, shared_down, experts, blocks, halves, False, f32, "shared_expert")
        return by_dp(out[0])

    def to_dp(kept, met, part=slice(None)):
        return [(kept[k, part].astype(f32) + met[k, part].astype(f32)).astype(bf16) for k in range(1, n_dp)]

    def owned(kept, met, came, part=slice(None)):
        whole = kept[0, part].astype(f32) + met[0, part].astype(f32)
        for value in came:
            whole = whole + value.astype(f32)
        return whole

    def of(values, part):
        return [value[part] for value in values]

    def together(*values):
        return lax.optimization_barrier(values)

    upper, lower = slice(None, count), slice(count, None)
    wide = widen(tokens, expert_ids, route_weight, experts)
    if planes == 4:
        inner = (plane == 1) | (plane == 2)
        cut = count * 3 // 4
        middle, outward = ((1, 2), (2, 1)), ((1, 0), (2, 3))
        row_own = over_row(wide)
        near = over_planes(wide, ((0, 1), (1, 0), (2, 3), (3, 2)))
        opposite = over_planes(wide, middle)
        kept_0, sent_0 = routed([wide, over_core(wide)])
        kept_0, near, opposite = together(kept_0, near, opposite)
        met_0 = over_core(sent_0)
        kept_0, met_0, row_own = together(kept_0, met_0, row_own)

        inputs = [row_own, near, over_core(row_own), over_core(near)]
        row_near = over_row(near)
        relay = jnp.where(inner, opposite, wide)
        next_ = over_planes(relay, ((0, 2), (3, 1), (1, 0), (2, 3)))
        came_0 = over_dp(to_dp(kept_0, met_0))
        *inputs, _ = together(*inputs, relay)
        kept_1, sent_1 = routed(inputs)
        kept_1, sent_1, row_near, next_, *came_0 = together(kept_1, sent_1, row_near, next_, *came_0)

        inputs = [row_near, next_, over_core(row_near), over_core(next_)]
        row_next = over_row(next_)
        met_1 = over_core(sent_1)
        sends = to_dp(kept_1, met_1)
        came_1 = over_dp(sends)
        relayed, *_ = together(next_, *sends)
        last = over_planes(relayed, outward)
        kept_2, sent_2 = routed(inputs)
        kept_2, sent_2, row_next, *came_1 = together(kept_2, sent_2, row_next, *came_1)
        kept_2, last = together(kept_2, last)

        far = jnp.where(inner, opposite, last)
        inputs = [row_next, far, over_core(row_next), over_core(far)]
        row_far = over_row(far)
        met_2 = over_core(sent_2)
        sends = to_dp(kept_2, met_2)
        came_2 = over_dp(sends)
        total_1, *_ = together(owned(kept_1, met_1, of(came_1, lower), lower).astype(bf16), *sends)
        home_1 = exchange(total_1, "expert", 4)
        kept_3, sent_3 = routed(inputs)
        kept_3, sent_3, row_far, home_1, *came_2 = together(kept_3, sent_3, row_far, home_1, *came_2)

        inputs = [row_far, over_core(row_far)]
        met_3 = over_core(sent_3)
        cross_1 = owned(kept_2, met_2, of(came_2, upper), upper).astype(bf16)
        total_2 = owned(kept_2, met_2, of(came_2, lower), lower).astype(bf16)
        home_2 = exchange(total_2[:cut], "expert", 8)
        came_3 = over_dp(to_dp(kept_3, met_3, upper))
        kept_4, sent_4 = routed(inputs)
        kept_4, sent_4, home_2, *came_3 = together(kept_4, sent_4, home_2, *came_3)

        met_4 = over_core(sent_4)
        last_rows = sends = [(kept_4[k].astype(f32) + met_4[k].astype(f32)).astype(bf16) for k in range(n_dp)]
        back_3 = [over_row(sends[0])] + [across_both(send, k) for k, send in enumerate(sends) if k]
        cross_2 = owned(kept_3, met_3, came_3, upper).astype(bf16)
        cross_2 = exchange(jnp.concatenate([cross_2, total_2[cut:]], axis=0), "expert", 8)
        *sends, cross_1, _ = together(*to_dp(kept_3, met_3, lower), cross_1, sends[0])
        cross_1 = exchange(cross_1, "expert", 4)
        came_far = over_dp(sends)
        rows, *_ = together(tokens, *last_rows)
        shared_part, cross_1, cross_2, *came = together(shared(rows), cross_1, cross_2, *back_3, *came_far)
        total_3 = owned(kept_3, met_3, came, lower)
        total_3 = total_3.astype(bf16)
        home_3 = exchange(total_3, "expert", 12)
        *sends, _ = together(*[shared_part[k].astype(bf16) for k in range(1, n_dp)], total_3)
        came_shared = over_dp(sends)
        cross = cross_1.astype(f32) + cross_2[:count].astype(f32)
        back_0 = over_row((owned(kept_1, met_1, of(came_1, upper), upper) + cross).astype(bf16))
        home_2 = jnp.concatenate([home_2, cross_2[count:]], axis=0)
        homes = [home_1, home_2, home_3]
        answer = owned(kept_0, met_0, came_0 + came_shared) + shared_part[0] + back_0.astype(f32)
    else:
        totals = []
        for s in range(planes):
            here = exchange(wide, "expert", 4 * s) if s else wide
            across = over_row(here)
            kept, sent = routed([here, across, over_core(here), over_core(across)])
            met = over_core(sent)
            whole = owned(kept, met, over_dp(to_dp(kept, met)))
            totals.append(whole[:count] + over_row(whole[count:].astype(bf16)).astype(f32))
        homes = [exchange(totals[s].astype(bf16), "expert", 4 * s) for s in range(1, planes)]
        shared_part = shared(tokens)
        answer = totals[0] + shared_part[0]
        for value in over_dp([shared_part[k].astype(bf16) for k in range(1, n_dp)]):
            answer = answer + value.astype(f32)
    for value in homes:
        answer = answer + value.astype(f32)
    return answer.astype(bf16)


def solution(mesh):
    in_specs = (
        P("expert", None),
        P("expert", None),
        P("expert", None),
        P(),
        P("expert", None, "dp"),
        P("expert", None, "dp"),
        P("expert", "dp", None),
        P(None, "dp"),
        P(None, "dp"),
        P("dp", None),
    )
    out_specs = P("expert", "dp")
    return jax.shard_map(local, mesh=mesh, in_specs=in_specs, out_specs=out_specs, check_vma=False)
```

```python
import functools

import jax
import jax.numpy as jnp
from jax import lax
from jax.experimental import pallas as pl
from jax.experimental.pallas import tpu as pltpu
from jax.sharding import PartitionSpec as P

routed_scale = 2.5
LANES = 128
SIDE = 256
AHEAD = 2
VMEM = 42 * 1024 * 1024


def exchange(value, axis, mask):
    pairs = [(source, source ^ mask) for source in range(lax.axis_size(axis))]
    return lax.ppermute(value, axis, pairs)


def widen_body(experts, tokens, ids, weight, rows):
    count, width = tokens.shape
    ids = jnp.transpose(ids[...])
    rates = jnp.transpose(weight[...])
    rates = routed_scale * rates / jnp.sum(rates, axis=1, keepdims=True)
    lane = lax.broadcasted_iota(jnp.int32, (count, LANES), 1)
    total = jnp.zeros((count, LANES), jnp.float32)
    for choice in range(ids.shape[1]):
        total += jnp.where(ids[:, choice : choice + 1] == lane % experts, rates[:, choice : choice + 1], 0.0)
    high = total.astype(jnp.bfloat16).astype(jnp.float32)
    middle = (total - high).astype(jnp.bfloat16).astype(jnp.float32)
    low = total - high - middle
    term = lane // experts
    held = jnp.where(term == 0, high, jnp.where(term == 1, middle, jnp.where(term == 2, low, 0.0)))
    rows[:, :width] = tokens[...]
    rows[:, width:] = held.astype(jnp.bfloat16)


def widen(tokens, ids, weight, experts):
    count, width = tokens.shape
    return pl.pallas_call(
        functools.partial(widen_body, experts),
        out_shape=jax.ShapeDtypeStruct((count, width + LANES), tokens.dtype),
        grid=(1,),
        in_specs=[pl.BlockSpec(array.shape, lambda i: (0, 0)) for array in (tokens, ids.T, weight.T)],
        out_specs=pl.BlockSpec((count, width + LANES), lambda i: (0, 0)),
        compiler_params=pltpu.CompilerParams(vmem_limit_bytes=16 * 1024 * 1024),
        name="widen",
    )(*[pltpu.with_memory_space_constraint(array, pltpu.HBM) for array in (tokens, ids.T, weight.T)])


def ffn_body(experts, blocks, out_rows, scaled, n_in, n_out, *refs):
    info = refs[0]
    inputs = refs[1 : 1 + n_in]
    gate, up, down = refs[1 + n_in : 4 + n_in]
    refs = refs[4 + n_in :]
    outs = refs[:n_out]
    x, gate_v, up_v, down_v, act, factor, result, x_sem, gate_sem, up_sem, down_sem, out_sem = refs[n_out:]
    width, hidden = gate.shape
    steps = hidden // SIDE
    tile = result.shape[2]
    per_block = width // blocks // tile
    dp = info[0]

    copies = []
    for number, source in enumerate(inputs):
        size = source.shape[0]
        copies.append(pltpu.make_async_copy(source, x.at[pl.ds(number * size, size), :], x_sem.at[number]))
    def side(weights, held, sems, j):
        return pltpu.make_async_copy(
            weights.at[:, pl.ds(pl.multiple_of(j * SIDE, SIDE), SIDE)], held.at[j], sems.at[j]
        )

    def lower(i):
        column = ((i // per_block) ^ dp if blocks > 1 else 0) * (width // blocks) + (i % per_block) * tile
        return pltpu.make_async_copy(
            down.at[:, pl.ds(pl.multiple_of(column, LANES), tile)], down_v.at[i], down_sem.at[i]
        )

    def leave(i):
        given = []
        for number, (first, count) in enumerate(out_rows):
            given.append(
                pltpu.make_async_copy(
                    result.at[i, pl.ds(first, count), :],
                    outs[number].at[i // per_block, :, pl.ds(pl.multiple_of((i % per_block) * tile, LANES), tile)],
                    out_sem.at[i, number],
                )
            )
        return given

    for copy in copies:
        copy.start()
    for j in range(min(AHEAD, steps)):
        side(gate, gate_v, gate_sem, j).start()
        side(up, up_v, up_sem, j).start()
    for copy in copies:
        copy.wait()

    if scaled:
        held = x[:, width:].astype(jnp.float32)
        lane = lax.broadcasted_iota(jnp.int32, held.shape, 1)
        chosen = jnp.sum(jnp.where(lane % experts == info[1], held, 0.0), axis=1, keepdims=True)
        factor[...] = jnp.broadcast_to(chosen, factor.shape)

    def lowers():
        for i in range(blocks * per_block):
            lower(i).start()

    if steps <= AHEAD:
        lowers()

    def first(j, carry):
        side(gate, gate_v, gate_sem, j).wait()
        side(up, up_v, up_sem, j).wait()

        @pl.when(j + AHEAD < steps)
        def _():
            side(gate, gate_v, gate_sem, j + AHEAD).start()
            side(up, up_v, up_sem, j + AHEAD).start()

        @pl.when(j + AHEAD == steps - 1)
        def _():
            lowers()

        rows = x[:, :width]
        gate_val = jnp.dot(rows, gate_v[j], preferred_element_type=jnp.float32)
        up_val = jnp.dot(rows, up_v[j], preferred_element_type=jnp.float32)
        value = gate_val / (1.0 + jnp.exp(-gate_val)) * up_val
        if scaled:
            value = value * factor[...]
        act[:, pl.ds(pl.multiple_of(j * SIDE, SIDE), SIDE)] = value.astype(act.dtype)
        return carry

    lax.fori_loop(0, steps, first, 0)

    def second(i, carry):
        lower(i).wait()
        value = jnp.dot(act[...], down_v[i], preferred_element_type=jnp.float32)
        result[i] = value.astype(result.dtype)
        for copy in leave(i):
            copy.start()
        return carry

    lax.fori_loop(0, blocks * per_block, second, 0)

    def finish(i, carry):
        for copy in leave(i):
            copy.wait()
        return carry

    lax.fori_loop(0, blocks * per_block, finish, 0)


def ffn(info, inputs, gate, up, down, experts, blocks, out_rows, scaled, dtype, name):
    width, hidden = gate.shape
    row_width = inputs[0].shape[1]
    rows = sum(count for _, count in out_rows)
    tiles = max(blocks, 2)
    tile = width // tiles
    steps = hidden // SIDE
    flops = 6 * rows * width * hidden
    body = functools.partial(ffn_body, experts, blocks, out_rows, scaled, len(inputs), len(out_rows))
    scratch = [
        pltpu.VMEM((rows, row_width), jnp.bfloat16),
        pltpu.VMEM((steps, width, SIDE), jnp.bfloat16),
        pltpu.VMEM((steps, width, SIDE), jnp.bfloat16),
        pltpu.VMEM((tiles, hidden, tile), jnp.bfloat16),
        pltpu.VMEM((rows, hidden), jnp.bfloat16),
        pltpu.VMEM((rows, SIDE), jnp.float32),
        pltpu.VMEM((tiles, rows, tile), dtype),
        pltpu.SemaphoreType.DMA((len(inputs),)),
        pltpu.SemaphoreType.DMA((steps,)),
        pltpu.SemaphoreType.DMA((steps,)),
        pltpu.SemaphoreType.DMA((tiles,)),
        pltpu.SemaphoreType.DMA((tiles, len(out_rows))),
    ]
    return pl.pallas_call(
        body,
        out_shape=[jax.ShapeDtypeStruct((blocks, count, width // blocks), dtype) for _, count in out_rows],
        in_specs=[pl.BlockSpec(memory_space=pltpu.SMEM)]
        + [pl.BlockSpec(memory_space=pl.ANY)] * (len(inputs) + 3),
        out_specs=[pl.BlockSpec(memory_space=pl.ANY)] * len(out_rows),
        scratch_shapes=scratch,
        compiler_params=pltpu.CompilerParams(vmem_limit_bytes=VMEM),
        cost_estimate=pl.CostEstimate(
            flops=flops, bytes_accessed=6 * width * hidden + 4 * rows * width, transcendentals=rows * hidden
        ),
        name=name,
    )(info, *inputs, *[pltpu.with_memory_space_constraint(array, pltpu.HBM) for array in (gate, up, down)])


def local(
    tokens,
    expert_ids,
    route_weight,
    pair_swap,
    expert_gate,
    expert_up,
    expert_down,
    shared_gate,
    shared_up,
    shared_down,
):
    count, width = tokens.shape
    experts = lax.axis_size("expert")
    n_dp = lax.axis_size("dp")
    half_axis = experts // 2
    column = lax.axis_index("expert")
    dp = lax.axis_index("dp")
    mine = jnp.where(pair_swap[column % half_axis] == 1, (column + half_axis) % experts, column)
    info = jnp.stack([dp, mine]).astype(jnp.int32)
    blocks = n_dp if (width // n_dp) % LANES == 0 else 1
    planes = experts // 4
    plane = column // 4
    f32, bf16 = jnp.float32, jnp.bfloat16
    weights = (expert_gate[0], expert_up[0], expert_down[0])
    def over_core(value):
        return exchange(value, "expert", 1)

    def over_row(value):
        return exchange(value, "expert", 2)

    def over_dp(sends):
        return [exchange(send, "dp", k + 1) for k, send in enumerate(sends)]

    def across_both(value, k):
        pairs = [(d * experts + e, (d ^ k) * experts + (e ^ 2)) for d in range(n_dp) for e in range(experts)]
        return lax.ppermute(value, ("dp", "expert"), pairs)

    def over_planes(value, pairs):
        return lax.ppermute(value, "expert", [(4 * s + k, 4 * t + k) for s, t in pairs for k in range(4)])

    def by_dp(value):
        if blocks == n_dp:
            return value
        rows = value.shape[1]
        parts = value.transpose(1, 0, 2).reshape(rows, n_dp, width // n_dp)
        return jnp.take(parts, dp ^ jnp.arange(n_dp), axis=1).transpose(1, 0, 2)

    def routed(inputs):
        half = len(inputs) // 2 * count
        halves = ((0, half), (half, half))
        kept, sent = ffn(info, inputs, *weights, experts, blocks, halves, True, bf16, "routed_expert")
        return by_dp(kept), by_dp(sent)

    def shared(rows):
        halves = ((0, count),)
        out = ffn(info, [rows], shared_gate, shared_up, shared_down, experts, blocks, halves, False, f32, "shared_expert")
        return by_dp(out[0])

    def to_dp(kept, met, part=slice(None)):
        return [(kept[k, part].astype(f32) + met[k, part].astype(f32)).astype(bf16) for k in range(1, n_dp)]

    def owned(kept, met, came, part=slice(None)):
        whole = kept[0, part].astype(f32) + met[0, part].astype(f32)
        for value in came:
            whole = whole + value.astype(f32)
        return whole

    def of(values, part):
        return [value[part] for value in values]

    def together(*values):
        return lax.optimization_barrier(values)

    upper, lower = slice(None, count), slice(count, None)
    wide = widen(tokens, expert_ids, route_weight, experts)
    if planes == 4:
        inner = (plane == 1) | (plane == 2)
        cut = count * 3 // 4
        middle, outward = ((1, 2), (2, 1)), ((1, 0), (2, 3))
        row_own = over_row(wide)
        near = over_planes(wide, ((0, 1), (1, 0), (2, 3), (3, 2)))
        opposite = over_planes(wide, middle)
        kept_0, sent_0 = routed([wide, over_core(wide)])
        kept_0, near, opposite = together(kept_0, near, opposite)
        met_0 = over_core(sent_0)
        kept_0, met_0, row_own = together(kept_0, met_0, row_own)

        inputs = [row_own, near, over_core(row_own), over_core(near)]
        row_near = over_row(near)
        relay = jnp.where(inner, opposite, wide)
        next_ = over_planes(relay, ((0, 2), (3, 1), (1, 0), (2, 3)))
        came_0 = over_dp(to_dp(kept_0, met_0))
        *inputs, _ = together(*inputs, relay)
        kept_1, sent_1 = routed(inputs)
        kept_1, sent_1, row_near, next_, *came_0 = together(kept_1, sent_1, row_near, next_, *came_0)

        inputs = [row_near, next_, over_core(row_near), over_core(next_)]
        row_next = over_row(next_)
        met_1 = over_core(sent_1)
        sends = to_dp(kept_1, met_1)
        came_1 = over_dp(sends)
        relayed, *_ = together(next_, *sends)
        last = over_planes(relayed, outward)
        kept_2, sent_2 = routed(inputs)
        kept_2, sent_2, row_next, *came_1 = together(kept_2, sent_2, row_next, *came_1)
        kept_2, last = together(kept_2, last)

        far = jnp.where(inner, opposite, last)
        inputs = [row_next, far, over_core(row_next), over_core(far)]
        row_far = over_row(far)
        met_2 = over_core(sent_2)
        sends = to_dp(kept_2, met_2)
        came_2 = over_dp(sends)
        total_1, *_ = together(owned(kept_1, met_1, of(came_1, lower), lower).astype(bf16), *sends)
        home_1 = exchange(total_1, "expert", 4)
        kept_3, sent_3 = routed(inputs)
        kept_3, sent_3, row_far, home_1, *came_2 = together(kept_3, sent_3, row_far, home_1, *came_2)

        inputs = [row_far, over_core(row_far)]
        met_3 = over_core(sent_3)
        cross_1 = owned(kept_2, met_2, of(came_2, upper), upper).astype(bf16)
        total_2 = owned(kept_2, met_2, of(came_2, lower), lower).astype(bf16)
        home_2 = exchange(total_2[:cut], "expert", 8)
        came_3 = over_dp(to_dp(kept_3, met_3, upper))
        kept_4, sent_4 = routed(inputs)
        kept_4, sent_4, home_2, *came_3 = together(kept_4, sent_4, home_2, *came_3)

        met_4 = over_core(sent_4)
        last_rows = sends = [(kept_4[k].astype(f32) + met_4[k].astype(f32)).astype(bf16) for k in range(n_dp)]
        back_3 = [over_row(sends[0])] + [across_both(send, k) for k, send in enumerate(sends) if k]
        cross_2 = owned(kept_3, met_3, came_3, upper).astype(bf16)
        cross_2 = exchange(jnp.concatenate([cross_2, total_2[cut:]], axis=0), "expert", 8)
        cross_1, _ = together(cross_1, sends[0])
        sends = to_dp(kept_3, met_3, lower)
        cross_1 = exchange(cross_1, "expert", 4)
        came_far = over_dp(sends)
        rows, *_ = together(tokens, *last_rows)
        early = owned(kept_0, met_0, came_0) + home_1.astype(f32)
        early, shared_part, cross_1, cross_2, *came = together(early, shared(rows), cross_1, cross_2, *back_3, *came_far)
        total_3 = owned(kept_3, met_3, came, lower)
        total_3 = total_3.astype(bf16)
        home_3 = exchange(total_3, "expert", 12)
        *sends, _ = together(*[shared_part[k].astype(bf16) for k in range(1, n_dp)], total_3)
        came_shared = over_dp(sends)
        cross = cross_1.astype(f32) + cross_2[:count].astype(f32)
        back_0 = over_row((owned(kept_1, met_1, of(came_1, upper), upper) + cross).astype(bf16))
        home_2 = jnp.concatenate([home_2, cross_2[count:]], axis=0)
        homes = [home_2, home_3]
        answer = early + shared_part[0] + back_0.astype(f32)
        for value in came_shared:
            answer = answer + value.astype(f32)
    else:
        totals = []
        for s in range(planes):
            here = exchange(wide, "expert", 4 * s) if s else wide
            across = over_row(here)
            kept, sent = routed([here, across, over_core(here), over_core(across)])
            met = over_core(sent)
            whole = owned(kept, met, over_dp(to_dp(kept, met)))
            totals.append(whole[:count] + over_row(whole[count:].astype(bf16)).astype(f32))
        homes = [exchange(totals[s].astype(bf16), "expert", 4 * s) for s in range(1, planes)]
        shared_part = shared(tokens)
        answer = totals[0] + shared_part[0]
        for value in over_dp([shared_part[k].astype(bf16) for k in range(1, n_dp)]):
            answer = answer + value.astype(f32)
    for value in homes:
        answer = answer + value.astype(f32)
    return answer.astype(bf16)


def solution(mesh):
    in_specs = (
        P("expert", None),
        P("expert", None),
        P("expert", None),
        P(),
        P("expert", None, "dp"),
        P("expert", None, "dp"),
        P("expert", "dp", None),
        P(None, "dp"),
        P(None, "dp"),
        P("dp", None),
    )
    out_specs = P("expert", "dp")
    return jax.shard_map(local, mesh=mesh, in_specs=in_specs, out_specs=out_specs, check_vma=False)
```

```python
import functools

import jax
import jax.numpy as jnp
from jax import lax
from jax.experimental import pallas as pl
from jax.experimental.pallas import tpu as pltpu
from jax.sharding import PartitionSpec as P

routed_scale = 2.5
LANES = 128
SIDE = 256
AHEAD = 2
VMEM = 42 * 1024 * 1024


def exchange(value, axis, mask):
    pairs = [(source, source ^ mask) for source in range(lax.axis_size(axis))]
    return lax.ppermute(value, axis, pairs)


def widen_body(experts, tokens, ids, weight, rows):
    count, width = tokens.shape
    ids = jnp.transpose(ids[...])
    rates = jnp.transpose(weight[...])
    rates = routed_scale * rates / jnp.sum(rates, axis=1, keepdims=True)
    lane = lax.broadcasted_iota(jnp.int32, (count, LANES), 1)
    total = jnp.zeros((count, LANES), jnp.float32)
    for choice in range(ids.shape[1]):
        total += jnp.where(ids[:, choice : choice + 1] == lane % experts, rates[:, choice : choice + 1], 0.0)
    high = total.astype(jnp.bfloat16).astype(jnp.float32)
    middle = (total - high).astype(jnp.bfloat16).astype(jnp.float32)
    low = total - high - middle
    term = lane // experts
    held = jnp.where(term == 0, high, jnp.where(term == 1, middle, jnp.where(term == 2, low, 0.0)))
    rows[:, :width] = tokens[...]
    rows[:, width:] = held.astype(jnp.bfloat16)


def widen(tokens, ids, weight, experts):
    count, width = tokens.shape
    return pl.pallas_call(
        functools.partial(widen_body, experts),
        out_shape=jax.ShapeDtypeStruct((count, width + LANES), tokens.dtype),
        grid=(1,),
        in_specs=[pl.BlockSpec(array.shape, lambda i: (0, 0)) for array in (tokens, ids.T, weight.T)],
        out_specs=pl.BlockSpec((count, width + LANES), lambda i: (0, 0)),
        compiler_params=pltpu.CompilerParams(vmem_limit_bytes=16 * 1024 * 1024),
        name="widen",
    )(*[pltpu.with_memory_space_constraint(array, pltpu.HBM) for array in (tokens, ids.T, weight.T)])


def ffn_body(experts, blocks, out_rows, scaled, n_in, n_out, *refs):
    info = refs[0]
    inputs = refs[1 : 1 + n_in]
    gate, up, down = refs[1 + n_in : 4 + n_in]
    refs = refs[4 + n_in :]
    outs = refs[:n_out]
    x, gate_v, up_v, down_v, act, factor, result, x_sem, gate_sem, up_sem, down_sem, out_sem = refs[n_out:]
    width, hidden = gate.shape
    steps = hidden // SIDE
    tile = result.shape[2]
    per_block = width // blocks // tile
    dp = info[0]

    copies = []
    for number, source in enumerate(inputs):
        size = source.shape[0]
        copies.append(pltpu.make_async_copy(source, x.at[pl.ds(number * size, size), :], x_sem.at[number]))
    def side(weights, held, sems, j):
        return pltpu.make_async_copy(
            weights.at[:, pl.ds(pl.multiple_of(j * SIDE, SIDE), SIDE)], held.at[j], sems.at[j]
        )

    def lower(i):
        column = ((i // per_block) ^ dp if blocks > 1 else 0) * (width // blocks) + (i % per_block) * tile
        return pltpu.make_async_copy(
            down.at[:, pl.ds(pl.multiple_of(column, LANES), tile)], down_v.at[i], down_sem.at[i]
        )

    def leave(i):
        given = []
        for number, (first, count) in enumerate(out_rows):
            given.append(
                pltpu.make_async_copy(
                    result.at[i, pl.ds(first, count), :],
                    outs[number].at[i // per_block, :, pl.ds(pl.multiple_of((i % per_block) * tile, LANES), tile)],
                    out_sem.at[i, number],
                )
            )
        return given

    for copy in copies:
        copy.start()
    for j in range(min(AHEAD, steps)):
        side(gate, gate_v, gate_sem, j).start()
        side(up, up_v, up_sem, j).start()
    for copy in copies:
        copy.wait()

    if scaled:
        held = x[:, width:].astype(jnp.float32)
        lane = lax.broadcasted_iota(jnp.int32, held.shape, 1)
        chosen = jnp.sum(jnp.where(lane % experts == info[1], held, 0.0), axis=1, keepdims=True)
        factor[...] = jnp.broadcast_to(chosen, factor.shape)

    def lowers():
        for i in range(blocks * per_block):
            lower(i).start()

    if steps <= AHEAD:
        lowers()

    def first(j, carry):
        side(gate, gate_v, gate_sem, j).wait()
        side(up, up_v, up_sem, j).wait()

        @pl.when(j + AHEAD < steps)
        def _():
            side(gate, gate_v, gate_sem, j + AHEAD).start()
            side(up, up_v, up_sem, j + AHEAD).start()

        @pl.when(j + AHEAD == steps - 1)
        def _():
            lowers()

        rows = x[:, :width]
        gate_val = jnp.dot(rows, gate_v[j], preferred_element_type=jnp.float32)
        up_val = jnp.dot(rows, up_v[j], preferred_element_type=jnp.float32)
        value = gate_val / (1.0 + jnp.exp(-gate_val)) * up_val
        if scaled:
            value = value * factor[...]
        act[:, pl.ds(pl.multiple_of(j * SIDE, SIDE), SIDE)] = value.astype(act.dtype)
        return carry

    lax.fori_loop(0, steps, first, 0)

    def second(i, carry):
        lower(i).wait()
        value = jnp.dot(act[...], down_v[i], preferred_element_type=jnp.float32)
        result[i] = value.astype(result.dtype)
        for copy in leave(i):
            copy.start()
        return carry

    lax.fori_loop(0, blocks * per_block, second, 0)

    def finish(i, carry):
        for copy in leave(i):
            copy.wait()
        return carry

    lax.fori_loop(0, blocks * per_block, finish, 0)


def ffn(info, inputs, gate, up, down, experts, blocks, out_rows, scaled, dtype, name):
    width, hidden = gate.shape
    row_width = inputs[0].shape[1]
    rows = sum(count for _, count in out_rows)
    tiles = max(blocks, 2)
    tile = width // tiles
    steps = hidden // SIDE
    flops = 6 * rows * width * hidden
    body = functools.partial(ffn_body, experts, blocks, out_rows, scaled, len(inputs), len(out_rows))
    scratch = [
        pltpu.VMEM((rows, row_width), jnp.bfloat16),
        pltpu.VMEM((steps, width, SIDE), jnp.bfloat16),
        pltpu.VMEM((steps, width, SIDE), jnp.bfloat16),
        pltpu.VMEM((tiles, hidden, tile), jnp.bfloat16),
        pltpu.VMEM((rows, hidden), jnp.bfloat16),
        pltpu.VMEM((rows, SIDE), jnp.float32),
        pltpu.VMEM((tiles, rows, tile), dtype),
        pltpu.SemaphoreType.DMA((len(inputs),)),
        pltpu.SemaphoreType.DMA((steps,)),
        pltpu.SemaphoreType.DMA((steps,)),
        pltpu.SemaphoreType.DMA((tiles,)),
        pltpu.SemaphoreType.DMA((tiles, len(out_rows))),
    ]
    return pl.pallas_call(
        body,
        out_shape=[jax.ShapeDtypeStruct((blocks, count, width // blocks), dtype) for _, count in out_rows],
        in_specs=[pl.BlockSpec(memory_space=pltpu.SMEM)]
        + [pl.BlockSpec(memory_space=pl.ANY)] * (len(inputs) + 3),
        out_specs=[pl.BlockSpec(memory_space=pl.ANY)] * len(out_rows),
        scratch_shapes=scratch,
        compiler_params=pltpu.CompilerParams(vmem_limit_bytes=VMEM),
        cost_estimate=pl.CostEstimate(
            flops=flops, bytes_accessed=6 * width * hidden + 4 * rows * width, transcendentals=rows * hidden
        ),
        name=name,
    )(info, *inputs, *[pltpu.with_memory_space_constraint(array, pltpu.HBM) for array in (gate, up, down)])


def local(
    tokens,
    expert_ids,
    route_weight,
    pair_swap,
    expert_gate,
    expert_up,
    expert_down,
    shared_gate,
    shared_up,
    shared_down,
):
    count, width = tokens.shape
    experts = lax.axis_size("expert")
    n_dp = lax.axis_size("dp")
    half_axis = experts // 2
    column = lax.axis_index("expert")
    dp = lax.axis_index("dp")
    mine = jnp.where(pair_swap[column % half_axis] == 1, (column + half_axis) % experts, column)
    info = jnp.stack([dp, mine]).astype(jnp.int32)
    blocks = n_dp if (width // n_dp) % LANES == 0 else 1
    planes = experts // 4
    plane = column // 4
    f32, bf16 = jnp.float32, jnp.bfloat16
    weights = (expert_gate[0], expert_up[0], expert_down[0])
    def over_core(value):
        return exchange(value, "expert", 1)

    def over_row(value):
        return exchange(value, "expert", 2)

    def over_dp(sends):
        return [exchange(send, "dp", k + 1) for k, send in enumerate(sends)]

    def across_both(value, k):
        pairs = [(d * experts + e, (d ^ k) * experts + (e ^ 2)) for d in range(n_dp) for e in range(experts)]
        return lax.ppermute(value, ("dp", "expert"), pairs)

    def over_planes(value, pairs):
        return lax.ppermute(value, "expert", [(4 * s + k, 4 * t + k) for s, t in pairs for k in range(4)])

    def by_dp(value):
        if blocks == n_dp:
            return value
        rows = value.shape[1]
        parts = value.transpose(1, 0, 2).reshape(rows, n_dp, width // n_dp)
        return jnp.take(parts, dp ^ jnp.arange(n_dp), axis=1).transpose(1, 0, 2)

    def routed(inputs):
        half = len(inputs) // 2 * count
        halves = ((0, half), (half, half))
        kept, sent = ffn(info, inputs, *weights, experts, blocks, halves, True, bf16, "routed_expert")
        return by_dp(kept), by_dp(sent)

    def shared(rows):
        halves = ((0, count),)
        out = ffn(info, [rows], shared_gate, shared_up, shared_down, experts, blocks, halves, False, f32, "shared_expert")
        return by_dp(out[0])

    def to_dp(kept, met, part=slice(None)):
        return [(kept[k, part].astype(f32) + met[k, part].astype(f32)).astype(bf16) for k in range(1, n_dp)]

    def owned(kept, met, came, part=slice(None)):
        whole = kept[0, part].astype(f32) + met[0, part].astype(f32)
        for value in came:
            whole = whole + value.astype(f32)
        return whole

    def of(values, part):
        return [value[part] for value in values]

    def together(*values):
        return lax.optimization_barrier(values)

    upper, lower = slice(None, count), slice(count, None)
    wide = widen(tokens, expert_ids, route_weight, experts)
    if planes == 4:
        inner = (plane == 1) | (plane == 2)
        cut = count * 3 // 4
        middle, outward = ((1, 2), (2, 1)), ((1, 0), (2, 3))
        row_own = over_row(wide)
        near = over_planes(wide, ((0, 1), (1, 0), (2, 3), (3, 2)))
        opposite = over_planes(wide, middle)
        kept_0, sent_0 = routed([wide, over_core(wide)])
        kept_0, near, opposite = together(kept_0, near, opposite)
        met_0 = over_core(sent_0)
        kept_0, met_0, row_own = together(kept_0, met_0, row_own)

        inputs = [row_own, near, over_core(row_own), over_core(near)]
        row_near = over_row(near)
        relay = jnp.where(inner, opposite, wide)
        next_ = over_planes(relay, ((0, 2), (3, 1), (1, 0), (2, 3)))
        came_0 = over_dp(to_dp(kept_0, met_0))
        *inputs, _ = together(*inputs, relay)
        kept_1, sent_1 = routed(inputs)
        kept_1, sent_1, row_near, next_, *came_0 = together(kept_1, sent_1, row_near, next_, *came_0)

        inputs = [row_near, next_, over_core(row_near), over_core(next_)]
        row_next = over_row(next_)
        met_1 = over_core(sent_1)
        sends = to_dp(kept_1, met_1)
        came_1 = over_dp(sends)
        relayed, *_ = together(next_, *sends)
        last = over_planes(relayed, outward)
        kept_2, sent_2 = routed(inputs)
        kept_2, sent_2, row_next, *came_1 = together(kept_2, sent_2, row_next, *came_1)
        kept_2, last = together(kept_2, last)

        far = jnp.where(inner, opposite, last)
        inputs = [row_next, far, over_core(row_next), over_core(far)]
        row_far = over_row(far)
        met_2 = over_core(sent_2)
        sends = to_dp(kept_2, met_2)
        came_2 = over_dp(sends)
        total_1, *_ = together(owned(kept_1, met_1, of(came_1, lower), lower).astype(bf16), *sends)
        home_1 = exchange(total_1, "expert", 4)
        kept_3, sent_3 = routed(inputs)
        kept_3, sent_3, row_far, home_1, *came_2 = together(kept_3, sent_3, row_far, home_1, *came_2)

        inputs = [row_far, over_core(row_far)]
        met_3 = over_core(sent_3)
        cross_1 = owned(kept_2, met_2, of(came_2, upper), upper).astype(bf16)
        total_2 = owned(kept_2, met_2, of(came_2, lower), lower).astype(bf16)
        home_2 = exchange(total_2[:cut], "expert", 8)
        came_3 = over_dp(to_dp(kept_3, met_3, upper))
        kept_4, sent_4 = routed(inputs)
        kept_4, sent_4, *came_3 = together(kept_4, sent_4, *came_3)
        home_2, *came_3 = together(home_2, *came_3)

        met_4 = over_core(sent_4)
        last_rows = sends = [(kept_4[k].astype(f32) + met_4[k].astype(f32)).astype(bf16) for k in range(n_dp)]
        back_3 = [over_row(sends[0])] + [across_both(send, k) for k, send in enumerate(sends) if k]
        cross_2 = owned(kept_3, met_3, came_3, upper).astype(bf16)
        cross_2 = exchange(jnp.concatenate([cross_2, total_2[cut:]], axis=0), "expert", 8)
        cross_1, _ = together(cross_1, sends[0])
        sends = to_dp(kept_3, met_3, lower)
        cross_1 = exchange(cross_1, "expert", 4)
        came_far = over_dp(sends)
        rows, *_ = together(tokens, *last_rows)
        early = owned(kept_0, met_0, came_0) + home_1.astype(f32)
        early, shared_part, cross_1, cross_2, *came = together(early, shared(rows), cross_1, cross_2, *back_3, *came_far)
        total_3 = owned(kept_3, met_3, came, lower)
        total_3 = total_3.astype(bf16)
        home_3 = exchange(total_3, "expert", 12)
        *sends, _ = together(*[shared_part[k].astype(bf16) for k in range(1, n_dp)], total_3)
        came_shared = over_dp(sends)
        cross = cross_1.astype(f32) + cross_2[:count].astype(f32)
        back_0 = over_row((owned(kept_1, met_1, of(came_1, upper), upper) + cross).astype(bf16))
        home_2 = jnp.concatenate([home_2, cross_2[count:]], axis=0)
        homes = [home_2, home_3]
        answer = early + shared_part[0] + back_0.astype(f32)
        for value in came_shared:
            answer = answer + value.astype(f32)
    else:
        totals = []
        for s in range(planes):
            here = exchange(wide, "expert", 4 * s) if s else wide
            across = over_row(here)
            kept, sent = routed([here, across, over_core(here), over_core(across)])
            met = over_core(sent)
            whole = owned(kept, met, over_dp(to_dp(kept, met)))
            totals.append(whole[:count] + over_row(whole[count:].astype(bf16)).astype(f32))
        homes = [exchange(totals[s].astype(bf16), "expert", 4 * s) for s in range(1, planes)]
        shared_part = shared(tokens)
        answer = totals[0] + shared_part[0]
        for value in over_dp([shared_part[k].astype(bf16) for k in range(1, n_dp)]):
            answer = answer + value.astype(f32)
    for value in homes:
        answer = answer + value.astype(f32)
    return answer.astype(bf16)


def solution(mesh):
    in_specs = (
        P("expert", None),
        P("expert", None),
        P("expert", None),
        P(),
        P("expert", None, "dp"),
        P("expert", None, "dp"),
        P("expert", "dp", None),
        P(None, "dp"),
        P(None, "dp"),
        P("dp", None),
    )
    out_specs = P("expert", "dp")
    return jax.shard_map(local, mesh=mesh, in_specs=in_specs, out_specs=out_specs, check_vma=False)
```

```python
import functools

import jax
import jax.numpy as jnp
from jax import lax
from jax.experimental import pallas as pl
from jax.experimental.pallas import tpu as pltpu
from jax.sharding import PartitionSpec as P

routed_scale = 2.5
LANES = 128
SIDE = 256
AHEAD = 2
VMEM = 42 * 1024 * 1024


def exchange(value, axis, mask):
    pairs = [(source, source ^ mask) for source in range(lax.axis_size(axis))]
    return lax.ppermute(value, axis, pairs)


def widen_body(experts, tokens, ids, weight, rows):
    count, width = tokens.shape
    ids = jnp.transpose(ids[...])
    rates = jnp.transpose(weight[...])
    rates = routed_scale * rates / jnp.sum(rates, axis=1, keepdims=True)
    lane = lax.broadcasted_iota(jnp.int32, (count, LANES), 1)
    total = jnp.zeros((count, LANES), jnp.float32)
    for choice in range(ids.shape[1]):
        total += jnp.where(ids[:, choice : choice + 1] == lane % experts, rates[:, choice : choice + 1], 0.0)
    high = total.astype(jnp.bfloat16).astype(jnp.float32)
    middle = (total - high).astype(jnp.bfloat16).astype(jnp.float32)
    low = total - high - middle
    term = lane // experts
    held = jnp.where(term == 0, high, jnp.where(term == 1, middle, jnp.where(term == 2, low, 0.0)))
    rows[:, :width] = tokens[...]
    rows[:, width:] = held.astype(jnp.bfloat16)


def widen(tokens, ids, weight, experts):
    count, width = tokens.shape
    return pl.pallas_call(
        functools.partial(widen_body, experts),
        out_shape=jax.ShapeDtypeStruct((count, width + LANES), tokens.dtype),
        grid=(1,),
        in_specs=[pl.BlockSpec(array.shape, lambda i: (0, 0)) for array in (tokens, ids.T, weight.T)],
        out_specs=pl.BlockSpec((count, width + LANES), lambda i: (0, 0)),
        compiler_params=pltpu.CompilerParams(vmem_limit_bytes=16 * 1024 * 1024),
        name="widen",
    )(*[pltpu.with_memory_space_constraint(array, pltpu.HBM) for array in (tokens, ids.T, weight.T)])


def ffn_body(experts, blocks, out_rows, scaled, n_in, n_out, *refs):
    info = refs[0]
    inputs = refs[1 : 1 + n_in]
    gate, up, down = refs[1 + n_in : 4 + n_in]
    refs = refs[4 + n_in :]
    outs = refs[:n_out]
    x, gate_v, up_v, down_v, act, factor, result, x_sem, gate_sem, up_sem, down_sem, out_sem = refs[n_out:]
    width, hidden = gate.shape
    steps = hidden // SIDE
    tile = result.shape[2]
    per_block = width // blocks // tile
    dp = info[0]

    copies = []
    for number, source in enumerate(inputs):
        size = source.shape[0]
        copies.append(pltpu.make_async_copy(source, x.at[pl.ds(number * size, size), :], x_sem.at[number]))
    def side(weights, held, sems, j):
        return pltpu.make_async_copy(
            weights.at[:, pl.ds(pl.multiple_of(j * SIDE, SIDE), SIDE)], held.at[j], sems.at[j]
        )

    def lower(i):
        column = ((i // per_block) ^ dp if blocks > 1 else 0) * (width // blocks) + (i % per_block) * tile
        return pltpu.make_async_copy(
            down.at[:, pl.ds(pl.multiple_of(column, LANES), tile)], down_v.at[i], down_sem.at[i]
        )

    def leave(i):
        given = []
        for number, (first, count) in enumerate(out_rows):
            given.append(
                pltpu.make_async_copy(
                    result.at[i, pl.ds(first, count), :],
                    outs[number].at[i // per_block, :, pl.ds(pl.multiple_of((i % per_block) * tile, LANES), tile)],
                    out_sem.at[i, number],
                )
            )
        return given

    for copy in copies:
        copy.start()
    for j in range(min(AHEAD, steps)):
        side(gate, gate_v, gate_sem, j).start()
        side(up, up_v, up_sem, j).start()
    for copy in copies:
        copy.wait()

    if scaled:
        held = x[:, width:].astype(jnp.float32)
        lane = lax.broadcasted_iota(jnp.int32, held.shape, 1)
        chosen = jnp.sum(jnp.where(lane % experts == info[1], held, 0.0), axis=1, keepdims=True)
        factor[...] = jnp.broadcast_to(chosen, factor.shape)

    def lowers():
        for i in range(blocks * per_block):
            lower(i).start()

    if steps <= AHEAD:
        lowers()

    def first(j, carry):
        side(gate, gate_v, gate_sem, j).wait()
        side(up, up_v, up_sem, j).wait()

        @pl.when(j + AHEAD < steps)
        def _():
            side(gate, gate_v, gate_sem, j + AHEAD).start()
            side(up, up_v, up_sem, j + AHEAD).start()

        @pl.when(j + AHEAD == steps - 1)
        def _():
            lowers()

        rows = x[:, :width]
        gate_val = jnp.dot(rows, gate_v[j], preferred_element_type=jnp.float32)
        up_val = jnp.dot(rows, up_v[j], preferred_element_type=jnp.float32)
        value = gate_val / (1.0 + jnp.exp(-gate_val)) * up_val
        if scaled:
            value = value * factor[...]
        act[:, pl.ds(pl.multiple_of(j * SIDE, SIDE), SIDE)] = value.astype(act.dtype)
        return carry

    lax.fori_loop(0, steps, first, 0)

    def second(i, carry):
        lower(i).wait()
        value = jnp.dot(act[...], down_v[i], preferred_element_type=jnp.float32)
        result[i] = value.astype(result.dtype)
        for copy in leave(i):
            copy.start()
        return carry

    lax.fori_loop(0, blocks * per_block, second, 0)

    def finish(i, carry):
        for copy in leave(i):
            copy.wait()
        return carry

    lax.fori_loop(0, blocks * per_block, finish, 0)


def ffn(info, inputs, gate, up, down, experts, blocks, out_rows, scaled, dtype, name):
    width, hidden = gate.shape
    row_width = inputs[0].shape[1]
    rows = sum(count for _, count in out_rows)
    tiles = max(blocks, 2)
    tile = width // tiles
    steps = hidden // SIDE
    flops = 6 * rows * width * hidden
    body = functools.partial(ffn_body, experts, blocks, out_rows, scaled, len(inputs), len(out_rows))
    scratch = [
        pltpu.VMEM((rows, row_width), jnp.bfloat16),
        pltpu.VMEM((steps, width, SIDE), jnp.bfloat16),
        pltpu.VMEM((steps, width, SIDE), jnp.bfloat16),
        pltpu.VMEM((tiles, hidden, tile), jnp.bfloat16),
        pltpu.VMEM((rows, hidden), jnp.bfloat16),
        pltpu.VMEM((rows, SIDE), jnp.float32),
        pltpu.VMEM((tiles, rows, tile), dtype),
        pltpu.SemaphoreType.DMA((len(inputs),)),
        pltpu.SemaphoreType.DMA((steps,)),
        pltpu.SemaphoreType.DMA((steps,)),
        pltpu.SemaphoreType.DMA((tiles,)),
        pltpu.SemaphoreType.DMA((tiles, len(out_rows))),
    ]
    return pl.pallas_call(
        body,
        out_shape=[jax.ShapeDtypeStruct((blocks, count, width // blocks), dtype) for _, count in out_rows],
        in_specs=[pl.BlockSpec(memory_space=pltpu.SMEM)]
        + [pl.BlockSpec(memory_space=pl.ANY)] * (len(inputs) + 3),
        out_specs=[pl.BlockSpec(memory_space=pl.ANY)] * len(out_rows),
        scratch_shapes=scratch,
        compiler_params=pltpu.CompilerParams(vmem_limit_bytes=VMEM),
        cost_estimate=pl.CostEstimate(
            flops=flops, bytes_accessed=6 * width * hidden + 4 * rows * width, transcendentals=rows * hidden
        ),
        name=name,
    )(info, *inputs, *[pltpu.with_memory_space_constraint(array, pltpu.HBM) for array in (gate, up, down)])


def local(
    tokens,
    expert_ids,
    route_weight,
    pair_swap,
    expert_gate,
    expert_up,
    expert_down,
    shared_gate,
    shared_up,
    shared_down,
):
    count, width = tokens.shape
    experts = lax.axis_size("expert")
    n_dp = lax.axis_size("dp")
    half_axis = experts // 2
    column = lax.axis_index("expert")
    dp = lax.axis_index("dp")
    mine = jnp.where(pair_swap[column % half_axis] == 1, (column + half_axis) % experts, column)
    info = jnp.stack([dp, mine]).astype(jnp.int32)
    blocks = n_dp if (width // n_dp) % LANES == 0 else 1
    planes = experts // 4
    plane = column // 4
    f32, bf16 = jnp.float32, jnp.bfloat16
    weights = (expert_gate[0], expert_up[0], expert_down[0])
    def over_core(value):
        return exchange(value, "expert", 1)

    def over_row(value):
        return exchange(value, "expert", 2)

    def over_dp(sends):
        return [exchange(send, "dp", k + 1) for k, send in enumerate(sends)]

    def across_both(value, k):
        pairs = [(d * experts + e, (d ^ k) * experts + (e ^ 2)) for d in range(n_dp) for e in range(experts)]
        return lax.ppermute(value, ("dp", "expert"), pairs)

    def over_planes(value, pairs):
        return lax.ppermute(value, "expert", [(4 * s + k, 4 * t + k) for s, t in pairs for k in range(4)])

    def by_dp(value):
        if blocks == n_dp:
            return value
        rows = value.shape[1]
        parts = value.transpose(1, 0, 2).reshape(rows, n_dp, width // n_dp)
        return jnp.take(parts, dp ^ jnp.arange(n_dp), axis=1).transpose(1, 0, 2)

    def routed(inputs):
        half = len(inputs) // 2 * count
        halves = ((0, half), (half, half))
        kept, sent = ffn(info, inputs, *weights, experts, blocks, halves, True, bf16, "routed_expert")
        return by_dp(kept), by_dp(sent)

    def shared(rows):
        halves = ((0, count),)
        out = ffn(info, [rows], shared_gate, shared_up, shared_down, experts, blocks, halves, False, f32, "shared_expert")
        return by_dp(out[0])

    def to_dp(kept, met, part=slice(None)):
        return [(kept[k, part].astype(f32) + met[k, part].astype(f32)).astype(bf16) for k in range(1, n_dp)]

    def owned(kept, met, came, part=slice(None)):
        whole = kept[0, part].astype(f32) + met[0, part].astype(f32)
        for value in came:
            whole = whole + value.astype(f32)
        return whole

    def of(values, part):
        return [value[part] for value in values]

    def together(*values):
        return lax.optimization_barrier(values)

    upper, lower = slice(None, count), slice(count, None)
    wide = widen(tokens, expert_ids, route_weight, experts)
    if planes == 4:
        inner = (plane == 1) | (plane == 2)
        cut = count * 3 // 4
        middle, outward = ((1, 2), (2, 1)), ((1, 0), (2, 3))
        row_own = over_row(wide)
        near = over_planes(wide, ((0, 1), (1, 0), (2, 3), (3, 2)))
        opposite = over_planes(wide, middle)
        kept_0, sent_0 = routed([wide, over_core(wide)])
        kept_0, near, opposite = together(kept_0, near, opposite)
        met_0 = over_core(sent_0)
        kept_0, met_0, row_own = together(kept_0, met_0, row_own)

        inputs = [row_own, near, over_core(row_own), over_core(near)]
        row_near = over_row(near)
        relay = jnp.where(inner, opposite, wide)
        next_ = over_planes(relay, ((0, 2), (3, 1), (1, 0), (2, 3)))
        came_0 = over_dp(to_dp(kept_0, met_0))
        *inputs, _ = together(*inputs, relay)
        kept_1, sent_1 = routed(inputs)
        kept_1, sent_1, row_near, next_, *came_0 = together(kept_1, sent_1, row_near, next_, *came_0)

        inputs = [row_near, next_, over_core(row_near), over_core(next_)]
        row_next = over_row(next_)
        met_1 = over_core(sent_1)
        sends = to_dp(kept_1, met_1)
        came_1 = over_dp(sends)
        relayed, *_ = together(next_, *sends)
        last = over_planes(relayed, outward)
        kept_2, sent_2 = routed(inputs)
        kept_2, sent_2, row_next, *came_1 = together(kept_2, sent_2, row_next, *came_1)
        kept_2, last = together(kept_2, last)

        far = jnp.where(inner, opposite, last)
        inputs = [row_next, far, over_core(row_next), over_core(far)]
        row_far = over_row(far)
        met_2 = over_core(sent_2)
        sends = to_dp(kept_2, met_2)
        came_2 = over_dp(sends)
        total_1, *_ = together(owned(kept_1, met_1, of(came_1, lower), lower).astype(bf16), *sends)
        home_1 = exchange(total_1, "expert", 4)
        kept_3, sent_3 = routed(inputs)
        kept_3, sent_3, home_1, *came_2 = together(kept_3, sent_3, home_1, *came_2)
        row_far, *came_2 = together(row_far, *came_2)

        inputs = [row_far, over_core(row_far)]
        met_3 = over_core(sent_3)
        cross_1 = owned(kept_2, met_2, of(came_2, upper), upper).astype(bf16)
        total_2 = owned(kept_2, met_2, of(came_2, lower), lower).astype(bf16)
        home_2 = exchange(total_2[:cut], "expert", 8)
        came_3 = over_dp(to_dp(kept_3, met_3, upper))
        kept_4, sent_4 = routed(inputs)
        kept_4, sent_4, *came_3 = together(kept_4, sent_4, *came_3)
        home_2, *came_3 = together(home_2, *came_3)

        met_4 = over_core(sent_4)
        last_rows = sends = [(kept_4[k].astype(f32) + met_4[k].astype(f32)).astype(bf16) for k in range(n_dp)]
        back_3 = [over_row(sends[0])] + [across_both(send, k) for k, send in enumerate(sends) if k]
        cross_2 = owned(kept_3, met_3, came_3, upper).astype(bf16)
        cross_2 = exchange(jnp.concatenate([cross_2, total_2[cut:]], axis=0), "expert", 8)
        cross_1, _ = together(cross_1, sends[0])
        sends = to_dp(kept_3, met_3, lower)
        cross_1 = exchange(cross_1, "expert", 4)
        came_far = over_dp(sends)
        rows, *_ = together(tokens, *last_rows)
        early = owned(kept_0, met_0, came_0) + home_1.astype(f32)
        early, shared_part, cross_1, cross_2, *came = together(early, shared(rows), cross_1, cross_2, *back_3, *came_far)
        total_3 = owned(kept_3, met_3, came, lower)
        total_3 = total_3.astype(bf16)
        home_3 = exchange(total_3, "expert", 12)
        *sends, _ = together(*[shared_part[k].astype(bf16) for k in range(1, n_dp)], total_3)
        came_shared = over_dp(sends)
        cross = cross_1.astype(f32) + cross_2[:count].astype(f32)
        back_0 = over_row((owned(kept_1, met_1, of(came_1, upper), upper) + cross).astype(bf16))
        home_2 = jnp.concatenate([home_2, cross_2[count:]], axis=0)
        homes = [home_2, home_3]
        answer = early + shared_part[0] + back_0.astype(f32)
        for value in came_shared:
            answer = answer + value.astype(f32)
    else:
        totals = []
        for s in range(planes):
            here = exchange(wide, "expert", 4 * s) if s else wide
            across = over_row(here)
            kept, sent = routed([here, across, over_core(here), over_core(across)])
            met = over_core(sent)
            whole = owned(kept, met, over_dp(to_dp(kept, met)))
            totals.append(whole[:count] + over_row(whole[count:].astype(bf16)).astype(f32))
        homes = [exchange(totals[s].astype(bf16), "expert", 4 * s) for s in range(1, planes)]
        shared_part = shared(tokens)
        answer = totals[0] + shared_part[0]
        for value in over_dp([shared_part[k].astype(bf16) for k in range(1, n_dp)]):
            answer = answer + value.astype(f32)
    for value in homes:
        answer = answer + value.astype(f32)
    return answer.astype(bf16)


def solution(mesh):
    in_specs = (
        P("expert", None),
        P("expert", None),
        P("expert", None),
        P(),
        P("expert", None, "dp"),
        P("expert", None, "dp"),
        P("expert", "dp", None),
        P(None, "dp"),
        P(None, "dp"),
        P("dp", None),
    )
    out_specs = P("expert", "dp")
    return jax.shard_map(local, mesh=mesh, in_specs=in_specs, out_specs=out_specs, check_vma=False)
```
